32 devices in a mesh: seq: 8 (over z, x), tp: 4 (over y, core).
Axes of the slice: x: 2, y: 2, z: 4, core: 2. Of those that a mesh axis runs over, the one named last changes fastest.
Arguments:
- tokens: bfloat16 [4096, 3072], P('seq', 'tp')
- norm_gain: float32 [3072], replicated, may hold values from 0.1 to 1.9
- w_query: bfloat16 [3072, 1536], P(None, 'tp'), as said below
- w_key: bfloat16 [3072, 1536], P(None, 'tp'), as said below
- w_value: bfloat16 [3072, 1536], P(None, 'tp'), may hold values from -0.109375 to 0.109375
- w_out: bfloat16 [1536, 3072], P('tp'), may hold values from -0.625 to 0.625
- final_gain: float32 [3072], P('tp'), may hold values from 0.1 to 1.9
- w_vocab: bfloat16 [3072, 32064], P('tp', 'seq'), may hold values from -0.3125 to 0.3125
- segment_ids: int32 [4096], P('seq'), may hold values from -1 to 7, as said below
- prompt_lengths: int32 [8], replicated, may hold values from 1 to 1024, as said below
- request_slots: int32 [128], replicated, may hold values from 0 to 3839, as said below
Outputs:
- kv_cache: bfloat16 [16, 4096, 192], P('tp', 'seq')
- hidden: bfloat16 [4096, 3072], P('seq', 'tp')
- hidden_norm: float32 [128], replicated
- top_logit: float32 [128], replicated
The draws below stay inside these ranges and needn't reach their ends.
Inputs may be any that keep to these rules, and one draw needn't show every extreme that they name: `segment_ids`: prompts 0 to 7 fill the slots in order from slot 0, prompt p on prompt_lengths[p] consecutive slots; all later slots are -1. `prompt_lengths`: they sum to 3840; the last prompt has exactly 1024 slots, and no prompt has more. `request_slots`: request r names a slot of prompt r // 16; the last request of each prompt names that prompt's final slot. `w_query`: Real-valued weights. `w_key`: Real-valued weights.
All inputs are finite; a program needn't handle non-finite values.
Results may differ from the reference program's by a relative error of at most 0.0095.
Values may be sent and summed in bfloat16 or wider, within the bound.
No kernel may reach another device: no remote copies, remote signals or barrier semaphores. Data moves between devices by JAX's collectives and lax.ppermute only.
A program may use at most 128 MiB of HBM per device.

```python
import math
import jax
import jax.numpy as jnp
from jax import lax

D = 3072
HEADS = 16
HD = 96
VOCAB = 32064
PROMPTS = 8
REQ_PER = 16
TOK_DEV = 512
TOKENS = 4096
MAXLEN = 1024
REQS = 128
N_TP = 4


def prompt_plan(key):
    base = jax.random.fold_in(key, 101)
    weights = jax.random.randint(jax.random.fold_in(base, 1), (PROMPTS - 1,), 500, 1001)
    remainder = TOKENS - TOK_DEV // 2 - MAXLEN
    others = remainder * weights // jnp.sum(weights)
    others = others.at[PROMPTS - 2].add(remainder - jnp.sum(others))
    order = jax.random.permutation(jax.random.fold_in(base, 2), PROMPTS - 1)
    others = others[order].astype(jnp.int32)
    return jnp.concatenate([others, jnp.full((1,), MAXLEN, jnp.int32)]).astype(jnp.int32)


def draw_prompt_lengths(key, part):
    return prompt_plan(key)


def draw_segment_ids(key, part):
    lengths = prompt_plan(key)
    ends = jnp.cumsum(lengths)
    slots = jnp.arange(TOKENS, dtype=jnp.int32)
    index = jnp.sum((slots[:, None] >= ends[None, :]).astype(jnp.int32), axis=1)
    return jnp.where(index >= PROMPTS, -1, index).astype(jnp.int32)


def draw_request_slots(key, part):
    lengths = prompt_plan(key)
    starts = jnp.cumsum(lengths) - lengths
    offsets = jax.random.randint(jax.random.fold_in(key, 202), (PROMPTS, REQ_PER), 0, lengths[:, None])
    offsets = offsets.at[:, REQ_PER - 1].set(lengths - 1)
    return (starts[:, None] + offsets).reshape(REQS).astype(jnp.int32)


def draw_tokens(key, part):
    column = jnp.arange(D, dtype=jnp.float32) / (D - 1)
    ramp = 0.5 * jnp.exp(column * math.log(4.0))
    values = jax.random.normal(jax.random.fold_in(key, 4), (TOKENS, D), jnp.float32)
    return (values * ramp[None, :]).astype(jnp.bfloat16)


def projection_pair(key):
    first = jax.random.normal(jax.random.fold_in(key, 31), (D, HEADS * HD), jnp.float32) * D ** (-0.5)
    second = jax.random.normal(jax.random.fold_in(key, 32), (D, HEADS * HD), jnp.float32) * D ** (-0.5)
    return (first, second)


def draw_w_query(key, part):
    return projection_pair(key)[0].astype(jnp.bfloat16)


def draw_w_key(key, part):
    return projection_pair(key)[1].astype(jnp.bfloat16)


def shard_levels(own_key, shape, pieces, least, high):
    gain, own = 1.0, jax.random.fold_in(own_key, 6)
    for axis_at, shards_of in pieces:
        heights = jnp.exp(jax.random.uniform(jax.random.fold_in(own, axis_at), (shards_of,), jnp.float32, least / len(pieces), high / len(pieces)))
        gain = gain * jnp.repeat(heights, shape[axis_at] // shards_of).reshape([-1 if axis == axis_at else 1 for axis in range(len(shape))])
    return gain


def centred(stream_key, dims, spread, reach, pieces=(), held_as=jnp.bfloat16):
    loudness = shard_levels(stream_key, dims, pieces, -0.22, 0.18) if pieces else 1.0
    values = jax.random.normal(stream_key, dims, jnp.float32) * spread * loudness
    return jnp.minimum(jnp.maximum(values, -reach), reach).astype(held_as)


def setup_inputs(seed: int = 0) -> dict:
    seeds = jax.random.split(jax.random.key(seed), 12)
    return {
        "tokens": draw_tokens(jax.random.fold_in(seeds[11], 71), 0),
        "norm_gain": jnp.clip(1.0 + 0.18 * jax.random.normal(seeds[1], (D,), jnp.float32), 0.1, 1.9),
        "w_query": draw_w_query(jax.random.fold_in(seeds[11], 71), 0),
        "w_key": draw_w_key(jax.random.fold_in(seeds[11], 71), 0),
        "w_value": centred(seeds[4], (D, HEADS * HD), D ** -0.5, 0.109375, ((1, 4),)),
        "w_out": centred(seeds[5], (HEADS * HD, D), (HEADS * HD // 16) ** -0.5, 0.625, ((0, 4),)),
        "final_gain": jnp.clip(1.0 + 0.18 * jax.random.normal(seeds[6], (D,), jnp.float32), 0.1, 1.9),
        "w_vocab": centred(seeds[7], (D, VOCAB), (D // 9) ** -0.5, 0.3125, ((0, 4), (1, 8))),
        "segment_ids": draw_segment_ids(jax.random.fold_in(seeds[11], 71), 0),
        "prompt_lengths": draw_prompt_lengths(jax.random.fold_in(seeds[11], 71), 0),
        "request_slots": draw_request_slots(jax.random.fold_in(seeds[11], 71), 0),
    }


NEG = -1e+30

def rotate(field, positions):
    middle = HD // 2
    inverse = 10000.0 ** (-(jnp.arange(middle, dtype=jnp.float32) * 2.0 / HD))
    angles = positions.astype(jnp.float32)[:, None] * inverse[None, :]
    cosine = jnp.cos(angles)[:, None, :]
    sine = jnp.sin(angles)[:, None, :]
    first = field[..., :middle]
    second = field[..., middle:]
    return jnp.concatenate([first * cosine - second * sine, second * cosine + first * sine], axis=-1)

def reference(tokens, norm_gain, w_query, w_key, w_value, w_out, final_gain, w_vocab, segment_ids, prompt_lengths, request_slots):
    wide = tokens.astype(jnp.float32)
    normed = (wide * lax.rsqrt(lax.optimization_barrier(jnp.mean(wide * wide, axis=-1, keepdims=True)) + 1e-05) * norm_gain).astype(jnp.bfloat16)
    starts = jnp.cumsum(prompt_lengths) - prompt_lengths
    matches = segment_ids[:, None] == jnp.arange(PROMPTS, dtype=jnp.int32)[None, :]
    first_slot = lax.optimization_barrier(jnp.sum(jnp.where(matches, starts[None, :], 0), axis=1)).astype(jnp.int32)
    slots = jnp.arange(TOKENS, dtype=jnp.int32)
    positions = jnp.where(segment_ids >= 0, slots - first_slot, 0).astype(jnp.int32)
    query = jnp.dot(normed, w_query, preferred_element_type=jnp.float32).reshape(TOKENS, HEADS, HD)
    key = jnp.dot(normed, w_key, preferred_element_type=jnp.float32).reshape(TOKENS, HEADS, HD)
    value = jnp.dot(normed, w_value, preferred_element_type=jnp.float32).reshape(TOKENS, HEADS, HD)
    rot_query = rotate(query, positions).astype(jnp.bfloat16)
    rot_key = rotate(key, positions).astype(jnp.bfloat16)
    paired = jnp.concatenate([rot_key, value.astype(jnp.bfloat16)], axis=-1)
    kv_cache = jnp.transpose(paired, (1, 0, 2))
    marks = jnp.where(segment_ids >= 0, segment_ids + 1, 0).astype(jnp.int32)
    padded_keys = jnp.concatenate([jnp.zeros((MAXLEN, HEADS, 2 * HD), jnp.bfloat16), paired], axis=0)
    padded_marks = jnp.concatenate([jnp.zeros((MAXLEN,), jnp.int32), marks], axis=0)
    scale = HD ** (-0.5)

    def one_block(index):
        begin = (index * TOK_DEV).astype(jnp.int32)
        query_block = lax.dynamic_slice_in_dim(rot_query, begin, TOK_DEV, 0).astype(jnp.float32)
        query_marks = lax.dynamic_slice_in_dim(marks, begin, TOK_DEV, 0)
        key_block = lax.dynamic_slice_in_dim(padded_keys, begin, MAXLEN + TOK_DEV, 0)
        key_marks = lax.dynamic_slice_in_dim(padded_marks, begin, MAXLEN + TOK_DEV, 0)
        keys = key_block[..., :HD].astype(jnp.float32)
        values = key_block[..., HD:].astype(jnp.float32)
        scores = jnp.einsum('qhd,khd->hqk', query_block, keys) * scale
        query_index = jnp.arange(TOK_DEV, dtype=jnp.int32)[:, None]
        key_index = jnp.arange(MAXLEN + TOK_DEV, dtype=jnp.int32)[None, :]
        allowed = (query_marks[:, None] == key_marks[None, :]) & (query_marks[:, None] > 0) & (key_index <= query_index + MAXLEN)
        masked = jnp.where(allowed[None], scores, NEG)
        largest = lax.optimization_barrier(jnp.max(masked, axis=-1))
        weights = jnp.where(allowed[None], jnp.exp(masked - largest[..., None]), 0.0)
        total = lax.optimization_barrier(jnp.sum(weights, axis=-1))
        rounded = lax.optimization_barrier(weights.astype(jnp.bfloat16)).astype(jnp.float32)
        numer = jnp.einsum('hqk,khd->hqd', rounded, values)
        attended = numer / jnp.where(total > 0, total, 1.0)[..., None]
        return jnp.transpose(attended, (1, 0, 2)).astype(jnp.bfloat16)
    blocks = lax.map(one_block, jnp.arange(TOKENS // TOK_DEV, dtype=jnp.int32))
    mixed = blocks.reshape(TOKENS, HEADS * HD)
    group_width = HEADS // N_TP * HD
    summed = jnp.zeros((TOKENS, D), jnp.float32)
    for group in range(N_TP):
        part_cols = mixed[:, group * group_width:(group + 1) * group_width]
        part_rows = w_out[group * group_width:(group + 1) * group_width]
        term = jnp.dot(part_cols, part_rows, preferred_element_type=jnp.float32).astype(jnp.bfloat16)
        summed = summed + lax.optimization_barrier(term).astype(jnp.float32)
    hidden_full = wide + summed
    hidden = hidden_full.astype(jnp.bfloat16)
    request_rows = hidden_full[request_slots]
    hidden_norm = jnp.sqrt(lax.optimization_barrier(jnp.mean(request_rows * request_rows, axis=-1)) + 1e-05)
    scaled_rows = request_rows * final_gain / hidden_norm[:, None]
    logits = jnp.dot(scaled_rows, w_vocab.astype(jnp.float32), precision=lax.Precision.HIGHEST)
    top_logit = lax.optimization_barrier(jnp.max(logits, axis=-1))
    return (kv_cache, hidden, hidden_norm, top_logit)
```

```python
from functools import partial

import jax
import jax.numpy as jnp
from jax import lax
from jax.experimental import pallas as pl
from jax.experimental.pallas import tpu as pltpu
from jax.sharding import PartitionSpec as P

D = 3072
HD = 96
EPS = 1e-05
NEG = -1e30
FAR = 2**30
SHRINK = 2.0**-16
F32 = jnp.float32
BF16 = jnp.bfloat16
VMEM_LIMIT = 48 * 1024 * 1024

WHOLE = pl.BlockSpec(memory_space=pltpu.VMEM)
SCALARS = pl.BlockSpec(memory_space=pltpu.SMEM)
ANYWHERE = pl.BlockSpec(memory_space=pl.ANY)


def call(body, outs, ins, scratch=(), flops=0, moved=0):
    return pl.pallas_call(
        body,
        out_shape=outs,
        in_specs=ins,
        out_specs=jax.tree.map(lambda _: WHOLE, outs),
        scratch_shapes=list(scratch),
        compiler_params=pltpu.CompilerParams(vmem_limit_bytes=VMEM_LIMIT),
        cost_estimate=pl.CostEstimate(flops=flops, bytes_accessed=moved, transcendentals=0),
    )


def struct(shape, dtype):
    return jax.ShapeDtypeStruct(shape, dtype)


def swap(array, axis, bit):
    count = lax.axis_size(axis)
    return lax.ppermute(array, axis, [(i, i ^ bit) for i in range(count)])


def shifted(array, axis, by):
    count = lax.axis_size(axis)
    pairs = [(i, i + by) for i in range(count) if 0 <= i + by < count]
    return lax.ppermute(array, axis, pairs)


def spread(array):
    far = swap(array, "tp", 2)
    near = swap(array, "tp", 1)
    return array, near, far, swap(far, "tp", 1)


def mm(a, b):
    return jnp.dot(a, b, preferred_element_type=F32)


def mm_t(a, b):
    return lax.dot_general(a, b, (((1,), (1,)), ((), ())), preferred_element_type=F32)


def rope(field, cosine, sine):
    width = field.shape[-1]
    lane = lax.broadcasted_iota(jnp.int32, field.shape, 1)
    first = lax.rem(lane, HD) < HD // 2
    partner = jnp.where(
        first, pltpu.roll(field, width - HD // 2, 1), pltpu.roll(field, HD // 2, 1)
    )
    return field * cosine + partner * sine


def project_body(kinds, mine, *refs):
    pieces = refs[:4]
    gain, cosine, sine = refs[4:7]
    count = len(kinds)
    weights = refs[7 : 7 + count]
    outs = refs[7 + count : -2]
    held, sems = refs[-2:]
    copies = [
        pltpu.make_async_copy(weights[i], held.at[i], sems.at[i]) for i in range(count)
    ]
    for copy in copies:
        copy.start()
    wide = [piece[...].astype(F32) for piece in pieces]
    squares = sum(jnp.sum(part * part, axis=1, keepdims=True) for part in wide)
    factor = lax.rsqrt(squares / D + EPS)
    width = wide[0].shape[1]
    normed = []
    places = []
    for b in range(4):
        block = mine[0] ^ b
        normed.append((wide[b] * factor * gain[pl.ds(block, 1), :]).astype(BF16))
        places.append(pl.ds(pl.multiple_of(block * width, width), width))
    for i, kind in enumerate(kinds):
        copies[i].wait()
        field = sum(mm(normed[b], held[i, places[b], :]) for b in range(4))
        if kind == "k":
            outs[0][:, : field.shape[1]] = rope(field, cosine[...], sine[...]).astype(BF16)
        elif kind == "v":
            outs[0][:, field.shape[1] :] = field.astype(BF16)
        else:
            outs[-1][...] = rope(field, cosine[...], sine[...]).astype(BF16)


def project(kinds, mine, pieces, gain, tables, weights):
    rows = pieces[0].shape[0]
    depth, width = weights[0].shape
    outs = []
    if "k" in kinds:
        outs.append(struct((rows, 2 * width), BF16))
    outs.append(struct((rows, width), BF16))
    return call(
        partial(project_body, kinds),
        outs,
        [SCALARS] + [WHOLE] * 7 + [ANYWHERE] * len(kinds),
        [
            pltpu.VMEM((len(kinds), depth, width), BF16),
            pltpu.SemaphoreType.DMA((len(kinds),)),
        ],
        flops=2 * rows * depth * width * len(kinds),
        moved=2 * depth * width * len(kinds) + 2 * rows * depth,
    )(mine, *pieces, gain, *tables, *weights)


def request_body(query, low, high, first, second, out):
    width = query.shape[1]
    heads = width // HD
    rows = query.shape[0]
    half = first.shape[0]
    pads = []
    for h in range(heads):
        at = slice(h * HD, (h + 1) * HD)
        v_at = slice(width + h * HD, width + (h + 1) * HD)
        scores = []
        allowed = []
        for i, block in enumerate((first, second)):
            key_slot = i * half + lax.broadcasted_iota(jnp.int32, (rows, half), 1)
            allowed.append((key_slot >= low[...]) & (key_slot <= high[...]))
            scores.append(
                jnp.where(allowed[i], mm_t(query[:, at], block[:, at]) * HD**-0.5, NEG)
            )
        largest = jnp.maximum(*[jnp.max(part, axis=1, keepdims=True) for part in scores])
        weights = [
            jnp.where(allowed[i], jnp.exp(scores[i] - largest), 0.0) for i in range(2)
        ]
        total = sum(jnp.sum(part, axis=1, keepdims=True) for part in weights)
        mixed = mm(weights[0].astype(BF16), first[:, v_at]) + mm(
            weights[1].astype(BF16), second[:, v_at]
        )
        filled = total > 0
        safe = jnp.where(filled, total, 1.0)
        out[:, at] = (mixed / safe).astype(BF16)
        pads.append(jnp.where(filled, largest + jnp.log(safe), NEG))
    out[:, width:] = pack_levels(pads)


def pack_levels(levels):
    rows = levels[0].shape[0]
    lane = lax.broadcasted_iota(jnp.int32, (rows, 128), 1)
    packed = jnp.zeros((rows, 128), F32)
    for h, level in enumerate(levels):
        for part in range(3):
            rounded = level.astype(BF16).astype(F32)
            packed = jnp.where(lane == 3 * h + part, rounded, packed)
            level = level - rounded
    return packed.astype(BF16)


def combine_body(flip, own, other, out):
    width = own.shape[1] - 128
    rows = own.shape[0]
    heads = width // HD
    turned = flip[0] > 0
    a = own[...].astype(F32)
    b = other[...].astype(F32)
    lower = jnp.where(turned, b, a)
    upper = jnp.where(turned, a, b)
    lane = lax.broadcasted_iota(jnp.int32, (rows, width), 1)
    share = jnp.zeros((rows, width), F32)
    rest = jnp.zeros((rows, width), F32)
    pads = []
    for h in range(heads):
        marks = []
        for side in (lower, upper):
            level = side[:, width + 3 * h : width + 3 * h + 1]
            for part in (1, 2):
                level = level + side[:, width + 3 * h + part : width + 3 * h + part + 1]
            marks.append(level)
        top = jnp.maximum(*marks)
        one, two = (jnp.exp(mark - top) for mark in marks)
        both = one + two
        pads.append(top + jnp.log(both))
        here = (lane >= h * HD) & (lane < (h + 1) * HD)
        share = jnp.where(here, one / both, share)
        rest = jnp.where(here, two / both, rest)
    out[:, :width] = (lower[:, :width] * share + upper[:, :width] * rest).astype(BF16)
    out[:, width:] = pack_levels(pads)


def combine(flip, own, other):
    return call(
        combine_body, struct(own.shape, BF16), [SCALARS, WHOLE, WHOLE], moved=3 * 2 * own.size
    )(flip, own, other)


def attend_body(distance, last, limits, query, low, block, *refs):
    if distance == 0:
        accum, largest, total = refs[-3:]
        accum[...] = jnp.zeros(accum.shape, F32)
        largest[...] = jnp.full(largest.shape, NEG, F32)
        total[...] = jnp.zeros(total.shape, F32)
    else:
        before = refs[:3]
        accum, largest, total = refs[-3:]
        accum[...] = before[0][...]
        largest[...] = before[1][...]
        total[...] = before[2][...]
    rows, width = query.shape
    heads = width // HD
    half = rows // 2
    lane = lax.broadcasted_iota(jnp.int32, (half, 128), 1)

    def visit(i, j):
        q_at = slice(i * half, (i + 1) * half)
        k_at = slice(j * half, (j + 1) * half)
        key_slot = (
            j * half - distance * rows + lax.broadcasted_iota(jnp.int32, (half, half), 1)
        )
        allowed = key_slot >= low[q_at, :]
        if distance == 0 and i == j:
            query_slot = i * half + lax.broadcasted_iota(jnp.int32, (half, half), 0)
            allowed = allowed & (key_slot <= query_slot)
        old_m = largest[q_at, :]
        old_t = total[q_at, :]
        new_m = old_m
        new_t = old_t
        for h in range(heads):
            at = slice(h * HD, (h + 1) * HD)
            v_at = slice(width + h * HD, width + (h + 1) * HD)
            scores = jnp.where(
                allowed, mm_t(query[q_at, at], block[k_at, at]) * HD**-0.5, NEG
            )
            m_h = old_m[:, h : h + 1]
            m_new = jnp.maximum(m_h, jnp.max(scores, axis=1, keepdims=True))
            weights = jnp.where(allowed, jnp.exp(scores - m_new), 0.0)
            factor = jnp.exp(m_h - m_new)
            t_new = old_t[:, h : h + 1] * factor + jnp.sum(weights, axis=1, keepdims=True)
            accum[q_at, at] = accum[q_at, at] * factor + mm(
                weights.astype(BF16), block[k_at, v_at]
            )
            new_m = jnp.where(lane == h, m_new, new_m)
            new_t = jnp.where(lane == h, t_new, new_t)
        largest[q_at, :] = new_m
        total[q_at, :] = new_t

    for i in range(2):
        for j in range(2):
            if distance == 0 and j > i:
                continue
            end = (j + 1) * half - distance * rows
            pl.when(limits[i] < end)(partial(visit, i, j))
    if last:
        out = refs[-4]
        for h in range(heads):
            at = slice(h * HD, (h + 1) * HD)
            t_h = total[:, h : h + 1]
            out[:, at] = (accum[:, at] / jnp.where(t_h > 0, t_h, 1.0)).astype(BF16)


def attend(distance, last, limits, query, low, block, state):
    rows, width = query.shape
    shapes = [struct((rows, width), F32), struct((rows, 128), F32), struct((rows, 128), F32)]
    scratch = []
    if last:
        scratch = [pltpu.VMEM(s.shape, s.dtype) for s in shapes]
        outs = struct((rows, width), BF16)
    else:
        outs = shapes
    return call(
        partial(attend_body, distance, last),
        outs,
        [SCALARS] + [WHOLE] * (3 + len(state)),
        scratch,
        flops=4 * rows * rows * width,
        moved=4 * rows * width * 6,
    )(limits, query, low, block, *state)


def rows_body(a0, a1, a2, a3, w0, w1, w2, w3, tokens, gain, vocab, out, squares, scaled):
    @pl.when(pl.program_id(0) == 0)
    def _():
        summed = sum(
            mm(a[...], w[...]).astype(BF16).astype(F32)
            for a, w in ((a0, w0), (a1, w1), (a2, w2), (a3, w3))
        )
        rows = tokens[...].astype(F32) + summed
        squares[...] = jnp.broadcast_to(
            jnp.sum(rows * rows, axis=1, keepdims=True), squares.shape
        )
        scaled[...] = (rows * (gain[...] * SHRINK)).astype(BF16)

    out[...] = mm(scaled[...], vocab[...]).astype(BF16)


def request_logits(parts, weights, tokens, gain, vocab):
    count, width = tokens.shape
    columns = vocab.shape[1]
    tile = 1024
    keep = lambda shape: pl.BlockSpec(shape, lambda i: (0, 0))
    return pl.pallas_call(
        rows_body,
        grid=(pl.cdiv(columns, tile),),
        out_shape=[struct((count, columns), BF16), struct((count, 128), F32)],
        in_specs=[keep(p.shape) for p in parts]
        + [keep(w.shape) for w in weights]
        + [keep(tokens.shape), keep(gain.shape), pl.BlockSpec((width, tile), lambda i: (0, i))],
        out_specs=[pl.BlockSpec((count, tile), lambda i: (0, i)), keep((count, 128))],
        scratch_shapes=[pltpu.VMEM((count, width), BF16)],
        compiler_params=pltpu.CompilerParams(vmem_limit_bytes=VMEM_LIMIT),
        cost_estimate=pl.CostEstimate(
            flops=2 * count * width * columns, bytes_accessed=2 * vocab.size, transcendentals=0
        ),
    )(*parts, *weights, tokens, gain, vocab)


def shards(
    tokens,
    norm_gain,
    w_query,
    w_key,
    w_value,
    w_out,
    final_gain,
    w_vocab,
    segment_ids,
    prompt_lengths,
    request_slots,
):
    rows, columns = tokens.shape
    half = rows // 2
    width = w_query.shape[1]
    heads = width // HD
    n_seq = lax.axis_size("seq")
    span = n_seq // 4
    seq_index = lax.axis_index("seq")
    tp_index = lax.axis_index("tp")
    base = seq_index * rows
    requests = request_slots.shape[0]

    inside = request_slots - base
    picks = (inside[:, None] == jnp.arange(rows, dtype=jnp.int32)[None, :]).astype(BF16)
    own_tokens = mm(picks, tokens).astype(BF16)
    near_tokens = own_tokens
    for by in range(1, span + 1):
        near_tokens = near_tokens + shifted(own_tokens, "seq", -by)

    pieces = [spread(tokens[:half]), spread(tokens[half:])]
    request_pieces = spread(near_tokens)

    starts = jnp.cumsum(prompt_lengths) - prompt_lengths
    prompts = prompt_lengths.shape[0]
    matches = segment_ids[:, None] == jnp.arange(prompts, dtype=jnp.int32)[None, :]
    first_slot = jnp.sum(jnp.where(matches, starts[None, :], 0), axis=1)
    slots = base + jnp.arange(rows, dtype=jnp.int32)
    valid = segment_ids >= 0
    positions = jnp.where(valid, slots - first_slot, 0)
    low = jnp.where(valid, first_slot - base, FAR)
    request_starts = jnp.repeat(starts, requests // prompts)
    request_low = request_starts - base
    request_positions = request_slots - request_starts

    lanes = jnp.arange(width, dtype=jnp.int32) % HD
    middle = HD // 2
    inverse = 10000.0 ** (-((lanes % middle).astype(F32) * 2.0 / HD))
    sign = jnp.where(lanes < middle, -1.0, 1.0)

    def tables(places):
        angles = places.astype(F32)[:, None] * inverse[None, :]
        return jnp.cos(angles), jnp.sin(angles) * sign[None, :]

    gain = norm_gain.reshape(4, columns)
    mine = tp_index.reshape(1)
    cosine, sine = tables(positions)
    kv = []
    query = []
    for i in range(2):
        at = slice(i * half, (i + 1) * half)
        kv_i, q_i = project(
            "kvq", mine, pieces[i], gain, (cosine[at], sine[at]), (w_key, w_value, w_query)
        )
        kv.append(kv_i)
        query.append(q_i)
    (request_query,) = project(
        "q", mine, request_pieces, gain, tables(request_positions), (w_query,)
    )

    behind = [
        [shifted(kv[i], "seq", by) for i in range(2)] for by in range(1, span + 1)
    ]

    mixed = call(
        request_body,
        struct((requests, width + 128), BF16),
        [WHOLE] * 5,
        flops=4 * requests * rows * width,
    )(request_query, request_low[:, None], inside[:, None], kv[0], kv[1])
    bit = 1
    while bit < n_seq:
        flip = ((seq_index & bit) > 0).astype(jnp.int32).reshape(1)
        mixed = combine(flip, mixed, swap(mixed, "seq", bit))
        bit *= 2
    request_mixed = spread(mixed[:, :width])

    all_tokens = own_tokens
    bit = 1
    while bit < n_seq:
        all_tokens = all_tokens + swap(all_tokens, "seq", bit)
        bit *= 2

    def columns_for(b):
        return lax.dynamic_slice_in_dim(w_out, (tp_index ^ b) * columns, columns, 1)

    w_late, _ = lax.optimization_barrier((w_out, pieces[1][2]))
    w_parts = [lax.dynamic_slice_in_dim(w_out, tp_index * columns, columns, 1)]
    for b in range(1, 4):
        part = lax.dynamic_slice_in_dim(w_late, (tp_index ^ b) * columns, columns, 1)
        w_parts.append(swap(part, "tp", b))

    logits, squares = request_logits(
        request_mixed, w_parts, all_tokens, final_gain[None, :], w_vocab
    )
    squares = squares[:, 0]
    half_rows = requests // 2
    core = tp_index & 1
    side = tp_index >> 1
    kept = lax.dynamic_slice_in_dim(logits, core * half_rows, half_rows, 0)
    sent = lax.dynamic_slice_in_dim(logits, (1 - core) * half_rows, half_rows, 0)
    kept = (kept.astype(F32) + swap(sent, "tp", 1).astype(F32)).astype(BF16)
    quarter = requests // 4
    sent = lax.dynamic_slice_in_dim(kept, (1 - side) * quarter, quarter, 0)
    kept = lax.dynamic_slice_in_dim(kept, side * quarter, quarter, 0)
    top = jnp.max(kept.astype(F32) + swap(sent, "tp", 2).astype(F32), axis=-1)
    place = core * half_rows + side * quarter
    best = lax.dynamic_update_slice(jnp.full((requests,), -jnp.inf, F32), top, (place,))
    bit = 1
    while bit < n_seq:
        best = jnp.maximum(best, swap(best, "seq", bit))
        bit *= 2
    pair = jnp.stack([best, squares])
    for bit in (2, 1):
        other = swap(pair, "tp", bit)
        pair = jnp.stack([jnp.maximum(pair[0], other[0]), pair[1] + other[1]])
    hidden_norm = jnp.sqrt(pair[1] / D + EPS)
    top_logit = pair[0] / hidden_norm * (1.0 / SHRINK)

    whole_kv = jnp.concatenate(kv, axis=0)
    whole_query = jnp.concatenate(query, axis=0)
    kv_cache = jnp.transpose(
        jnp.concatenate(
            [whole_kv[:, :width].reshape(rows, heads, HD), whole_kv[:, width:].reshape(rows, heads, HD)],
            axis=-1,
        ),
        (1, 0, 2),
    )
    limits = jnp.stack([low[0], low[half]])
    state = attend(0, False, limits, whole_query, low[:, None], whole_kv, ())
    for by in range(1, span + 1):
        block = jnp.concatenate(behind[by - 1], axis=0)
        state = attend(by, by == span, limits, whole_query, low[:, None], block, state)
    attended = spread(state)
    summed = sum(
        mm(part, w).astype(BF16).astype(F32) for part, w in zip(attended, w_parts)
    )
    hidden = (tokens.astype(F32) + summed).astype(BF16)
    return (kv_cache, hidden, hidden_norm, top_logit)


def solution(mesh):
    return jax.shard_map(
        shards,
        mesh=mesh,
        in_specs=(
            P("seq", "tp"),
            P(),
            P(None, "tp"),
            P(None, "tp"),
            P(None, "tp"),
            P("tp", None),
            P("tp"),
            P("tp", "seq"),
            P("seq"),
            P(),
            P(),
        ),
        out_specs=(P("tp", "seq", None), P("seq", "tp"), P(), P()),
        check_vma=False,
    )
```

```python
from functools import partial

import jax
import jax.numpy as jnp
from jax import lax
from jax.experimental import pallas as pl
from jax.experimental.pallas import tpu as pltpu
from jax.sharding import PartitionSpec as P

D = 3072
HD = 96
EPS = 1e-05
NEG = -1e30
FLOOR = -5e29
NEVER = 2**30
LEVEL_ROWS = 16
SHRINK = 2.0**-16
DAMP = 2.0**-24
F32 = jnp.float32
BF16 = jnp.bfloat16
VMEM_LIMIT = 12 * 1024 * 1024

SCALARS = pl.BlockSpec(memory_space=pltpu.SMEM)
ANYWHERE = pl.BlockSpec(memory_space=pl.ANY)
FAR_MEMORY = pl.BlockSpec(memory_space=pltpu.HBM)


WHOLE = pl.BlockSpec(memory_space=pltpu.VMEM)


def call(body, outs, scalars, arrays, after=(), scratch=(), length=0, far=()):
    return pl.pallas_call(
        body,
        out_shape=outs,
        in_specs=[SCALARS] * len(scalars)
        + [FAR_MEMORY] * len(far)
        + [WHOLE] * len(arrays)
        + [ANYWHERE] * len(after),
        out_specs=[WHOLE] * len(outs),
        scratch_shapes=list(scratch),
        compiler_params=pltpu.CompilerParams(vmem_limit_bytes=VMEM_LIMIT),
        cost_estimate=pl.CostEstimate(
            flops=length * 10**9, bytes_accessed=0, transcendentals=0
        ),
    )(*scalars, *far, *arrays, *after)


def struct(shape, dtype):
    return jax.ShapeDtypeStruct(shape, dtype)


def swap(array, axis, bit):
    count = lax.axis_size(axis)
    return lax.ppermute(array, axis, [(i, i ^ bit) for i in range(count)])


def shifted(array, axis, by):
    count = lax.axis_size(axis)
    pairs = [(i, i + by) for i in range(count) if 0 <= i + by < count]
    return lax.ppermute(array, axis, pairs)


def spread(array):
    far = swap(array, "tp", 2)
    near = swap(array, "tp", 1)
    return array, near, far, swap(far, "tp", 1)


def mm(a, b):
    return jnp.dot(a, b, preferred_element_type=F32)


def mm_first(a, b):
    return lax.dot_general(a, b, (((0,), (0,)), ((), ())), preferred_element_type=F32)


def project_body(blocks, first, last, *refs):
    refs = list(refs)
    take = lambda count: [refs.pop(0) for _ in range(count)]
    mine = refs.pop(0)
    base = refs.pop(0) if last else None
    weights = take(3)
    (gain,) = take(1)
    pieces = take(len(blocks))
    accum, squares = take(2) if not first else (None, None)
    cosine, sine, asked = take(3) if last else (None, None, None)
    held, sems = refs[-2:]
    del refs[-2:]
    rows, part = pieces[0].shape
    width = weights[0].shape[1]
    copies = []
    for i in range(3):
        for j, block in enumerate(blocks):
            at = pl.ds(pl.multiple_of((mine[0] ^ block) * part, part), part)
            copies.append(
                pltpu.make_async_copy(weights[i].at[at, :], held.at[i, j], sems.at[i, j])
            )
    for copy in copies:
        copy.start()
    wide = [piece[...].astype(F32) for piece in pieces]
    total = sum(jnp.sum(w * w, axis=1, keepdims=True) for w in wide)
    if not first:
        total = total + squares[...]
    scaled = [
        (w * (gain[pl.ds(mine[0] ^ block, 1), :] * DAMP)).astype(BF16)
        for block, w in zip(blocks, wide)
    ]
    factor = lax.rsqrt(total / D + EPS) * (1.0 / DAMP)
    middle = HD // 2
    for i in range(3):
        at = slice(i * width, (i + 1) * width)
        field = 0.0
        for j, x in enumerate(scaled):
            copies[i * len(blocks) + j].wait()
            field = field + mm(x, held[i, j])
        if not first:
            field = field + accum[:, at]
        if not last:
            refs[-2][:, at] = field
            continue
        field = (field * factor).T
        kv, query, own = refs[-3:]
        for h in range(width // HD):
            at = h * HD
            a = field[at : at + middle]
            b = field[at + middle : at + HD]
            if i == 1:
                kv[2 * at + HD : 2 * at + 2 * HD, :] = field[at : at + HD].astype(BF16)
            else:
                to, out = (2 * at, kv) if i == 0 else (at, query)
                out[to : to + middle, :] = (a * cosine[...] - b * sine[...]).astype(BF16)
                out[to + middle : to + HD, :] = (b * cosine[...] + a * sine[...]).astype(BF16)
    if last:
        row = base[0] + lax.broadcasted_iota(jnp.int32, (rows, asked.shape[1]), 0)
        own[...] = mm(query[...], (asked[...] == row).astype(BF16)).astype(BF16)
    else:
        refs[-1][...] = total


def project(blocks, mine, gain, pieces, weights, before=(), ending=None, after=(), length=0):
    rows = pieces[0].shape[0]
    width = weights[0].shape[1]
    scalars, arrays = [mine], [gain, *pieces, *before]
    if ending is None:
        outs = [struct((rows, 3 * width), F32), struct((rows, 1), F32)]
    else:
        base, cosine, sine, asked = ending
        scalars.append(base)
        arrays += [cosine, sine, asked]
        outs = [
            struct((2 * width, rows), BF16),
            struct((width, rows), BF16),
            struct((width, asked.shape[1]), BF16),
        ]
    body = partial(project_body, blocks, not before, ending is not None)
    scratch = [
        pltpu.VMEM((3, len(blocks), pieces[0].shape[1], width), BF16),
        pltpu.SemaphoreType.DMA((3, len(blocks))),
    ]
    return call(body, outs, scalars, arrays, after, scratch, length, weights)


def copy_body(source, *refs):
    refs[-1][...] = source[...]


def pick_body(base, slots, tokens, out):
    rows = tokens.shape[0]
    count = slots.shape[1]
    row = base[0] + lax.broadcasted_iota(jnp.int32, (rows, count), 0)
    out[...] = mm_first((slots[...] == row).astype(BF16), tokens[...]).astype(BF16)


def request_body(count, low, high, block, *refs):
    out = refs[-1]
    query = sum(part[...] for part in refs[:count])
    width, rows = query.shape
    half = block.shape[1] // 2
    allowed = []
    for i in range(2):
        key_slot = i * half + lax.broadcasted_iota(jnp.int32, (half, rows), 0)
        allowed.append((key_slot >= low[...]) & (key_slot <= high[...]))
    results = []
    levels = []
    for h in range(width // HD):
        at = slice(h * HD, (h + 1) * HD)
        k_at = slice(2 * h * HD, (2 * h + 1) * HD)
        v_at = slice((2 * h + 1) * HD, (2 * h + 2) * HD)
        scores = [
            jnp.where(
                allowed[i], mm_first(block[k_at, i * half : (i + 1) * half], query[at, :]) * HD**-0.5, NEG
            )
            for i in range(2)
        ]
        largest = jnp.maximum(*[jnp.max(part, axis=0, keepdims=True) for part in scores])
        largest = jnp.maximum(largest, FLOOR)
        weights = [jnp.exp(part - largest) for part in scores]
        total = sum(jnp.sum(part, axis=0, keepdims=True) for part in weights)
        mixed = sum(
            mm(block[v_at, i * half : (i + 1) * half], weights[i].astype(BF16)) for i in range(2)
        )
        filled = total > 0
        safe = jnp.where(filled, total, 1.0)
        results.append((mixed * (1.0 / safe)).astype(BF16))
        levels.append(jnp.where(filled, largest + jnp.log(safe), NEG))
    for h, result in enumerate(results):
        out[h * HD : (h + 1) * HD, :] = result
    out[width:, :] = pack_levels(levels)


def pack_levels(levels):
    row = lax.broadcasted_iota(jnp.int32, (LEVEL_ROWS, levels[0].shape[1]), 0)
    packed = jnp.zeros(row.shape, F32)
    for h, level in enumerate(levels):
        for part in range(3):
            rounded = level.astype(BF16).astype(F32)
            packed = jnp.where(row == 3 * h + part, rounded, packed)
            level = level - rounded
    return packed.astype(BF16)


def combine_body(flip, own, other, *refs):
    out = refs[-1]
    width = own.shape[0] - LEVEL_ROWS
    turned = flip[0] > 0
    a = own[...].astype(F32)
    b = other[...].astype(F32)
    lower = jnp.where(turned, b, a)
    upper = jnp.where(turned, a, b)
    levels = []
    results = []
    for h in range(width // HD):
        marks = []
        for side in (lower, upper):
            at = width + 3 * h
            marks.append(side[at : at + 1] + side[at + 1 : at + 2] + side[at + 2 : at + 3])
        top = jnp.maximum(*marks)
        one, two = (jnp.exp(mark - top) for mark in marks)
        both = one + two
        levels.append(top + jnp.log(both))
        at = slice(h * HD, (h + 1) * HD)
        results.append((lower[at] * (one / both) + upper[at] * (two / both)).astype(BF16))
    for h, result in enumerate(results):
        out[h * HD : (h + 1) * HD, :] = result
    out[width:, :] = pack_levels(levels)


def combine(flip, own, other, after=()):
    return call(
        combine_body, [struct(own.shape, BF16)], [flip], [own, other], after
    )[0]


def attend_body(distances, last, low, query, *refs):
    width, rows = query.shape
    half = rows // 2
    heads = width // HD
    blocks = refs[: len(distances)]
    state = refs[len(distances) :]
    accum, largest, total = refs[-3:]
    if distances[0] == 0:
        accum[...] = jnp.zeros(accum.shape, F32)
        largest[...] = jnp.full(largest.shape, FLOOR, F32)
        total[...] = jnp.zeros(total.shape, F32)
    else:
        accum[...] = state[0][...]
        largest[...] = state[1][...]
        total[...] = state[2][...]

    def visit(distance, block, i, j):
        q_at = slice(i * half, (i + 1) * half)
        k_half = slice(j * half, (j + 1) * half)
        offset = j * half - distance * rows
        key_slot = offset + lax.broadcasted_iota(jnp.int32, (half, half), 0)
        allowed = key_slot >= low[:, q_at]
        if distance == 0 and i == j:
            query_slot = i * half + lax.broadcasted_iota(jnp.int32, (half, half), 1)
            allowed = allowed & (key_slot <= query_slot)
        done = []
        for h in range(heads):
            at = slice(h * HD, (h + 1) * HD)
            k_at = slice(2 * h * HD, (2 * h + 1) * HD)
            v_at = slice((2 * h + 1) * HD, (2 * h + 2) * HD)
            scores = mm_first(block[k_at, k_half], query[at, q_at]) * HD**-0.5
            scores = jnp.where(allowed, scores, NEG)
            m_old = largest[h : h + 1, q_at]
            m_new = jnp.maximum(m_old, jnp.max(scores, axis=0, keepdims=True))
            weights = jnp.exp(scores - m_new)
            factor = jnp.exp(m_old - m_new)
            t_new = total[h : h + 1, q_at] * factor + jnp.sum(weights, axis=0, keepdims=True)
            mixed = accum[at, q_at] * factor + mm(block[v_at, k_half], weights.astype(BF16))
            done.append((m_new, t_new, mixed))
        for h, (m_new, t_new, mixed) in enumerate(done):
            accum[h * HD : (h + 1) * HD, q_at] = mixed
            largest[h : h + 1, q_at] = m_new
            total[h : h + 1, q_at] = t_new

    limits = [jnp.min(low[:, i * half : (i + 1) * half]) for i in range(2)]
    for distance, block in zip(distances, blocks):
        for i in range(2):
            for j in range(2):
                if distance == 0 and j > i:
                    continue
                end = (j + 1) * half - distance * rows
                pl.when(limits[i] < end)(partial(visit, distance, block, i, j))
    if last:
        out = refs[-4]
        for h in range(heads):
            at = slice(h * HD, (h + 1) * HD)
            t_h = total[h : h + 1, :]
            accum[at, :] = accum[at, :] * (1.0 / jnp.where(t_h > 0, t_h, 1.0))
        out[...] = accum[...].T.astype(BF16)


def attend(distances, last, low, query, blocks, state=(), length=0):
    width, rows = query.shape
    shapes = [struct((width, rows), F32), struct((8, rows), F32), struct((8, rows), F32)]
    scratch = []
    outs = shapes
    if last:
        scratch = [pltpu.VMEM(s.shape, s.dtype) for s in shapes]
        outs = [struct((rows, width), BF16)]
    return call(
        partial(attend_body, distances, last),
        outs,
        [],
        [low, query, *blocks, *state],
        (),
        scratch,
        length,
    )


def logits_body(limit, tile, start, *refs):
    parts, weights = refs[:4], refs[4:8]
    tokens, gain, vocab = refs[8:11]
    sent, kept, squares, scaled = refs[-4:]
    step = pl.program_id(0)

    @pl.when(step == 0)
    def _():
        summed = sum(
            mm_first(a[...], w[...]).astype(BF16).astype(F32) for a, w in zip(parts, weights)
        )
        rows = tokens[...].astype(F32) + summed
        turned = rows.T
        squares[...] = jnp.sum(turned * turned, axis=0, keepdims=True)
        scaled[...] = (rows * (gain[...] * SHRINK)).T.astype(BF16)

    first = lax.rem(start[0] + step, 4) * tile
    row = first + lax.broadcasted_iota(jnp.int32, sent.shape, 0)
    logits = jnp.where(row < limit, mm(vocab[...], scaled[...]), NEG).astype(BF16)

    @pl.when(step < 2)
    def _():
        sent[...] = logits

    @pl.when(step >= 2)
    def _():
        kept[...] = logits


def request_logits(start, parts, weights, tokens, gain, vocab, after):
    limit, width = vocab.shape
    count = tokens.shape[0]
    tile = pl.cdiv(limit, 4 * 32) * 32
    keep = lambda a: pl.BlockSpec(a.shape, lambda i, start: (0, 0))
    return pl.pallas_call(
        partial(logits_body, limit, tile),
        grid_spec=pltpu.PrefetchScalarGridSpec(
            num_scalar_prefetch=1,
            grid=(4,),
            in_specs=[keep(a) for a in (*parts, *weights, tokens, gain)]
            + [pl.BlockSpec((tile, width), lambda i, start: (lax.rem(start[0] + i, 4), 0))]
            + [ANYWHERE] * len(after),
            out_specs=[
                pl.BlockSpec((tile, count), lambda i, start: (jnp.minimum(i, 1), 0)),
                pl.BlockSpec((tile, count), lambda i, start: (jnp.maximum(i - 2, 0), 0)),
                pl.BlockSpec((1, count), lambda i, start: (0, 0)),
            ],
            scratch_shapes=[pltpu.VMEM((width, count), BF16)],
        ),
        out_shape=[
            struct((2 * tile, count), BF16),
            struct((2 * tile, count), BF16),
            struct((1, count), F32),
        ],
        compiler_params=pltpu.CompilerParams(vmem_limit_bytes=VMEM_LIMIT),
        cost_estimate=pl.CostEstimate(flops=0, bytes_accessed=0, transcendentals=0),
    )(start, *parts, *weights, tokens, gain, vocab, *after)


def fold_body(side, kept, came, send, keep):
    quarter = send.shape[0]
    for out, turn in ((send, 1 - side[0]), (keep, side[0])):
        at = pl.ds(pl.multiple_of(turn * quarter, 16), quarter)
        out[...] = (kept[at, :].astype(F32) + came[at, :].astype(F32)).astype(out.dtype)


def top_body(kept, came, *refs):
    out = refs[-1]
    out[...] = jnp.max(kept[...] + came[...].astype(F32), axis=0, keepdims=True)


def split_body(mine, whole, *refs):
    outs = refs[-4:]
    width = outs[0].shape[1]
    for b in range(4):
        at = pl.ds(pl.multiple_of((mine[0] ^ b) * width, width), width)
        outs[b][...] = whole[:, at]


def shards(
    tokens,
    norm_gain,
    w_query,
    w_key,
    w_value,
    w_out,
    final_gain,
    w_vocab,
    segment_ids,
    prompt_lengths,
    request_slots,
):
    rows, columns = tokens.shape
    half = rows // 2
    width = w_query.shape[1]
    heads = width // HD
    n_seq = lax.axis_size("seq")
    span = n_seq // 4
    seq_index = lax.axis_index("seq")
    tp_index = lax.axis_index("tp")
    mine = tp_index.reshape(1)
    base = seq_index * rows
    requests = request_slots.shape[0]

    far = swap(tokens, "tp", 2)
    pieces = [tokens, swap(tokens, "tp", 1), far]
    gain = norm_gain.reshape(4, columns)
    weights = [
        pltpu.with_memory_space_constraint(w, pltpu.HBM) for w in (w_key, w_value, w_query)
    ]
    sums = project((0, 1), mine, gain, pieces[:2], weights)
    (relayed,) = call(copy_body, [struct(far.shape, BF16)], [], [far], sums[1:])
    pieces.append(swap(relayed, "tp", 1))

    inside = request_slots - base
    asked = request_slots[None, :]
    (own_tokens,) = call(
        pick_body, [struct((requests, columns), BF16)], [base.reshape(1)], [asked, tokens]
    )
    all_tokens = [own_tokens]
    bit = 1
    while bit < n_seq:
        all_tokens.append(all_tokens[-1] + swap(all_tokens[-1], "seq", bit))
        bit *= 2

    starts = jnp.cumsum(prompt_lengths) - prompt_lengths
    prompts = prompt_lengths.shape[0]
    matches = segment_ids[:, None] == jnp.arange(prompts, dtype=jnp.int32)[None, :]
    first_slot = jnp.sum(jnp.where(matches, starts[None, :], 0), axis=1)
    slots = base + jnp.arange(rows, dtype=jnp.int32)
    valid = segment_ids >= 0
    positions = jnp.where(valid, slots - first_slot, 0)
    low = jnp.where(valid, first_slot - base, NEVER)
    request_low = jnp.repeat(starts, requests // prompts) - base

    inverse = 10000.0 ** (-(jnp.arange(HD // 2, dtype=F32) * 2.0 / HD))

    def tables(places):
        angles = inverse[:, None] * places.astype(F32)[None, :]
        return jnp.cos(angles), jnp.sin(angles)

    cosine, sine = tables(positions)
    sums = project(
        (2,), mine, gain, pieces[2:3], weights, sums, None, all_tokens[2:3], length=10
    )
    kv, query, own_query = project(
        (3,),
        mine,
        gain,
        pieces[3:],
        weights,
        sums,
        (base.reshape(1), cosine, sine, asked),
    )
    asking = [own_query] + [shifted(own_query, "seq", -by) for by in range(1, span + 1)]

    kv_cache = jnp.transpose(kv.reshape(heads, 2 * HD, rows), (0, 2, 1))
    behind = shifted(kv, "seq", 1)

    own_state = attend((0,), False, low[None, :], query, (kv,))

    (mixed,) = call(
        partial(request_body, len(asking)),
        [struct((width + LEVEL_ROWS, requests), BF16)],
        [],
        [request_low[None, :], inside[None, :], kv, *asking],
        (all_tokens[-1], own_state[1]),
    )
    w_parts = call(
        split_body,
        [struct((width, columns), BF16)] * 4,
        [mine],
        [w_out],
        (mixed,),
    )
    w_split = w_parts[0]
    w_parts = [w_split] + [swap(w_parts[b], "tp", b) for b in range(1, 4)]

    afters = [[], [w_split], w_parts[1:2]]
    stages = [mixed]
    bit = 1
    while bit < n_seq:
        flip = ((seq_index & bit) > 0).astype(jnp.int32).reshape(1)
        after = afters.pop(0) if afters else ()
        stages.append(combine(flip, stages[-1], swap(stages[-1], "seq", bit), after))
        bit *= 2
    mixed = stages[-1]
    (later_kv,) = call(copy_body, [struct(kv.shape, BF16)], [], [kv], (mixed,))
    request_mixed = spread(mixed[:width])

    core = tp_index & 1
    side = tp_index >> 1
    sent, kept, squares = request_logits(
        (2 * (1 - core)).reshape(1),
        request_mixed,
        w_parts,
        all_tokens[-1],
        final_gain[None, :],
        pltpu.with_memory_space_constraint(w_vocab.T, pltpu.HBM),
        (),
    )
    quarter = kept.shape[0] // 2
    sent, kept = call(
        fold_body,
        [struct((quarter, requests), BF16), struct((quarter, requests), F32)],
        [side.reshape(1)],
        [kept, swap(sent, "tp", 1)],
    )
    blocks = [behind] + [shifted(later_kv, "seq", by) for by in range(2, span + 1)]
    distances = list(range(1, span + 1))
    state = own_state
    while distances:
        last = len(distances) <= 3
        state = attend(distances[:3], last, low[None, :], query, blocks[:3], state, 30)
        distances, blocks = distances[3:], blocks[3:]
    (best,) = call(
        top_body, [struct((1, requests), F32)], [], [kept, swap(sent, "tp", 2)], state[:1]
    )
    bit = 1
    while bit < n_seq:
        best = jnp.maximum(best, swap(best, "seq", bit))
        bit *= 2
    pair = jnp.concatenate([best, squares])
    for bit in (2, 1):
        other = swap(pair, "tp", bit)
        pair = jnp.stack([jnp.maximum(pair[0], other[0]), pair[1] + other[1]])
    hidden_norm = jnp.sqrt(pair[1] / D + EPS)
    top_logit = pair[0] / hidden_norm * (1.0 / SHRINK)

    attended = spread(state[0])
    summed = sum(
        mm(part, w).astype(BF16).astype(F32) for part, w in zip(attended, w_parts)
    )
    hidden = (tokens.astype(F32) + summed).astype(BF16)
    return (kv_cache, hidden, hidden_norm, top_logit)


def solution(mesh):
    return jax.shard_map(
        shards,
        mesh=mesh,
        in_specs=(
            P("seq", "tp"),
            P(),
            P(None, "tp"),
            P(None, "tp"),
            P(None, "tp"),
            P("tp", None),
            P("tp"),
            P("tp", "seq"),
            P("seq"),
            P(),
            P(),
        ),
        out_specs=(P("tp", "seq", None), P("seq", "tp"), P(), P()),
        check_vma=False,
    )
```

```python
from functools import partial

import jax
import jax.numpy as jnp
import numpy as np
from jax import lax
from jax.experimental import pallas as pl
from jax.experimental.pallas import tpu as pltpu
from jax.sharding import PartitionSpec as P

D = 3072
HD = 96
EPS = 1e-05
NEG = -1e30
FLOOR = -5e29
NEVER = 2**30
LEVEL_ROWS = 16
SHRINK = 2.0**-16
DAMP = 2.0**-24
LOG2_E = 1.4426950408889634
F32 = jnp.float32
BF16 = jnp.bfloat16
VMEM_LIMIT = 12 * 1024 * 1024

SCALARS = pl.BlockSpec(memory_space=pltpu.SMEM)
ANYWHERE = pl.BlockSpec(memory_space=pl.ANY)
FAR_MEMORY = pl.BlockSpec(memory_space=pltpu.HBM)


WHOLE = pl.BlockSpec(memory_space=pltpu.VMEM)


def whole(array):
    return pl.BlockSpec(array.shape, lambda i: (0, 0), pipeline_mode=pl.Buffered(1))


def call(body, outs, scalars, arrays, after=(), scratch=(), length=0, far=(), blocked=False):
    return pl.pallas_call(
        body,
        grid=(1,) if blocked else (),
        out_shape=outs,
        in_specs=[SCALARS] * len(scalars)
        + [FAR_MEMORY] * len(far)
        + [whole(array) if blocked else WHOLE for array in arrays]
        + [ANYWHERE] * len(after),
        out_specs=[whole(out) if blocked else WHOLE for out in outs],
        scratch_shapes=list(scratch),
        compiler_params=pltpu.CompilerParams(vmem_limit_bytes=VMEM_LIMIT),
        cost_estimate=pl.CostEstimate(
            flops=length * 10**9, bytes_accessed=0, transcendentals=0
        ),
    )(*scalars, *far, *arrays, *after)


def pinned(arrays):
    return [pltpu.with_memory_space_constraint(a, pltpu.HBM) for a in arrays]


def struct(shape, dtype):
    return jax.ShapeDtypeStruct(shape, dtype)


def swap(array, axis, bit):
    count = lax.axis_size(axis)
    return lax.ppermute(array, axis, [(i, i ^ bit) for i in range(count)])


def shifted(array, axis, by):
    count = lax.axis_size(axis)
    pairs = [(i, i + by) for i in range(count) if 0 <= i + by < count]
    return lax.ppermute(array, axis, pairs)


def spread(array):
    far = swap(array, "tp", 2)
    near = swap(array, "tp", 1)
    return array, near, far, swap(far, "tp", 1)


def mm(a, b):
    return jnp.dot(a, b, preferred_element_type=F32)


def mm_last(a, b):
    return lax.dot_general(a, b, (((1,), (1,)), ((), ())), preferred_element_type=F32)


def mm_first(a, b):
    return lax.dot_general(a, b, (((0,), (0,)), ((), ())), preferred_element_type=F32)


AHEAD = ((2, (0, 1, 2)), (3, (0, 1)), (3, (2,)))


def project_body(blocks, first, last, kinds, *refs):
    refs = list(refs)
    take = lambda count: [refs.pop(0) for _ in range(count)]
    mine = refs.pop(0)
    base = refs.pop(0) if last else None
    weights = take(3 if first else 1)
    (gain,) = take(1)
    pieces = take(len(blocks))
    accum, squares = take(2) if not first else (None, None)
    cosine, sine, asked = take(3) if last else (None, None, None)
    if first:
        held, sems = refs[-2:]
        del refs[-2:]
    rows, part = pieces[0].shape
    width = weights[0].shape[-1]
    copies = []
    onward = []
    if first:
        split_columns(mine, refs.pop(0), refs[-7:-3])
        for (block, needed), out in zip(AHEAD, refs[-3:]):
            at = pl.ds(pl.multiple_of((mine[0] ^ block) * part, part), part)
            onward += [
                pltpu.make_async_copy(weights[i].at[at, :], out.at[j], sems.at[i, block])
                for j, i in enumerate(needed)
            ]
        del refs[-7:]
    for i in range(3 if first else 0):
        for j, block in enumerate(blocks):
            at = pl.ds(pl.multiple_of((mine[0] ^ block) * part, part), part)
            copies.append(
                pltpu.make_async_copy(weights[i].at[at, :], held.at[i, j], sems.at[i, j])
            )
    for copy in copies + onward:
        copy.start()
    wide = [piece[...].astype(F32) for piece in pieces]
    total = sum(jnp.sum(w * w, axis=1, keepdims=True) for w in wide)
    if not first:
        total = total + squares[...]
    scaled = [
        (w * (gain[pl.ds(mine[0] ^ block, 1), :] * DAMP)).astype(BF16)
        for block, w in zip(blocks, wide)
    ]
    factor = lax.rsqrt(total / D + EPS) * (1.0 / DAMP)
    middle = HD // 2
    for i in kinds:
        place = kinds.index(i)
        at = slice(place * width, (place + 1) * width)
        field = 0.0
        for j, x in enumerate(scaled):
            if first:
                copies[i * len(blocks) + j].wait()
                field = field + mm(x, held[i, j])
            else:
                field = field + mm(x, weights[0][place])
        if not first:
            field = field + accum[:, at]
        if first:
            refs[-2][:, at] = field
            continue
        if not last:
            out = refs[-4] if i < 2 else refs[-2]
            out[:, at if i < 2 else slice(0, width)] = field
            continue
        field = (field * factor).T
        if 2 in kinds:
            query, own = refs[-2:]
        else:
            kv = refs[-1]
        for h in range(width // HD):
            at = h * HD
            a = field[at : at + middle]
            b = field[at + middle : at + HD]
            if i == 1:
                kv[2 * at + HD : 2 * at + 2 * HD, :] = field[at : at + HD].astype(BF16)
            else:
                to, out = (at, query) if i == 2 else (2 * at, kv)
                out[to : to + middle, :] = (a * cosine[...] - b * sine[...]).astype(BF16)
                out[to + middle : to + HD, :] = (b * cosine[...] + a * sine[...]).astype(BF16)
    if last and 2 in kinds:
        row = base[0] + lax.broadcasted_iota(jnp.int32, (rows, asked.shape[1]), 0)
        own[...] = mm(query[...], (asked[...] == row).astype(BF16)).astype(BF16)
    if not last:
        refs[-1][...] = total
        if not first:
            refs[-3][...] = total
    for copy in onward:
        copy.wait()


def project(
    blocks,
    mine,
    gain,
    pieces,
    weights,
    before=(),
    ending=None,
    after=(),
    length=0,
    kinds=(0, 1, 2),
    w_out=None,
):
    rows = pieces[0].shape[0]
    width = weights[0].shape[-1]
    scalars, arrays = [mine], [gain, *pieces, *before]
    if ending is None:
        outs = [struct((rows, 3 * width), F32), struct((rows, 1), F32)]
        if before:
            outs = [struct((rows, 2 * width), F32), struct((rows, 1), F32)]
            outs += [struct((rows, width), F32), struct((rows, 1), F32)]
    if not before:
        arrays.append(w_out)
        outs += [struct((w_out.shape[1] // 4, w_out.shape[0]), BF16)] * 4
        outs += [struct((len(n), pieces[0].shape[1], width), BF16) for _, n in AHEAD]
    if ending is not None:
        base, cosine, sine, asked = ending
        scalars.append(base)
        arrays += [cosine, sine, asked]
        outs = [struct((2 * width, rows), BF16)]
        if 2 in kinds:
            outs = [struct((width, rows), BF16), struct((width, asked.shape[1]), BF16)]
    body = partial(project_body, blocks, not before, ending is not None, kinds)
    if before:
        arrays = list(weights) + arrays
        return call(body, outs, scalars, arrays, after, length=length)
    scratch = [
        pltpu.VMEM((3, len(blocks), pieces[0].shape[1], width), BF16),
        pltpu.SemaphoreType.DMA((3, 4)),
    ]
    return call(body, outs, scalars, arrays, after, scratch, length, weights)


def copy_body(source, *refs):
    refs[-1][...] = source[...]


def prepare_body(base, lengths, segments, inverse, cosine, sine, low, asked_low):
    prompts = lengths.shape[0]
    rows = segments.shape[1]
    segment = segments[...]
    asked = lax.broadcasted_iota(jnp.int32, asked_low.shape, 1)
    each = asked_low.shape[1] // prompts
    first = jnp.zeros((1, rows), jnp.int32)
    asked_first = jnp.zeros(asked_low.shape, jnp.int32)
    start = jnp.int32(0)
    for p in range(prompts):
        first = jnp.where(segment == p, start, first)
        asked_first = jnp.where(
            (asked >= p * each) & (asked < (p + 1) * each), start, asked_first
        )
        start = start + lengths[p]
    valid = segment >= 0
    slot = base[0] + lax.broadcasted_iota(jnp.int32, (1, rows), 1)
    position = jnp.where(valid, slot - first, 0).astype(F32)
    angles = inverse[...] * position
    cosine[...] = jnp.cos(angles)
    sine[...] = jnp.sin(angles)
    low[...] = jnp.where(valid, first - base[0], NEVER)
    asked_low[...] = asked_first - base[0]


def pick_body(base, slots, tokens, out):
    rows = tokens.shape[0]
    count = slots.shape[1]
    row = base[0] + lax.broadcasted_iota(jnp.int32, (rows, count), 0)
    out[...] = mm_first(tokens[...], (slots[...] == row).astype(BF16)).astype(BF16)


def add_body(first, second, *refs):
    refs[-1][...] = first[...] + second[...]


def request_body(count, low, high, block, *refs):
    out = refs[-1]
    query = sum(part[...] for part in refs[:count])
    width, rows = query.shape
    half = block.shape[1] // 2
    allowed = []
    for i in range(2):
        key_slot = i * half + lax.broadcasted_iota(jnp.int32, (half, rows), 0)
        allowed.append((key_slot >= low[...]) & (key_slot <= high[...]))
    results = []
    levels = []
    for h in range(width // HD):
        at = slice(h * HD, (h + 1) * HD)
        k_at = slice(2 * h * HD, (2 * h + 1) * HD)
        v_at = slice((2 * h + 1) * HD, (2 * h + 2) * HD)
        scores = [
            jnp.where(
                allowed[i], mm_first(block[k_at, i * half : (i + 1) * half], query[at, :]) * HD**-0.5, NEG
            )
            for i in range(2)
        ]
        largest = jnp.maximum(*[jnp.max(part, axis=0, keepdims=True) for part in scores])
        largest = jnp.maximum(largest, FLOOR)
        weights = [jnp.exp(part - largest) for part in scores]
        total = sum(jnp.sum(part, axis=0, keepdims=True) for part in weights)
        mixed = sum(
            mm(block[v_at, i * half : (i + 1) * half], weights[i].astype(BF16)) for i in range(2)
        )
        filled = total > 0
        safe = jnp.where(filled, total, 1.0)
        results.append((mixed * (1.0 / safe)).astype(BF16))
        levels.append(jnp.where(filled, largest + jnp.log(safe), NEG))
    for h, result in enumerate(results):
        out[h * HD : (h + 1) * HD, :] = result
    out[width:, :] = pack_levels(levels)


def pack_levels(levels):
    row = lax.broadcasted_iota(jnp.int32, (LEVEL_ROWS, levels[0].shape[1]), 0)
    packed = jnp.zeros(row.shape, F32)
    for h, level in enumerate(levels):
        for part in range(3):
            rounded = level.astype(BF16).astype(F32)
            packed = jnp.where(row == 3 * h + part, rounded, packed)
            level = level - rounded
    return packed.astype(BF16)


def combine_body(flip, own, other, *refs):
    out = refs[-1]
    width = own.shape[0] - LEVEL_ROWS
    turned = flip[0] > 0
    a = own[...].astype(F32)
    b = other[...].astype(F32)
    lower = jnp.where(turned, b, a)
    upper = jnp.where(turned, a, b)
    levels = []
    results = []
    for h in range(width // HD):
        marks = []
        for side in (lower, upper):
            at = width + 3 * h
            marks.append(side[at : at + 1] + side[at + 1 : at + 2] + side[at + 2 : at + 3])
        top = jnp.maximum(*marks)
        one, two = (jnp.exp(mark - top) for mark in marks)
        both = one + two
        levels.append(top + jnp.log(both))
        at = slice(h * HD, (h + 1) * HD)
        results.append((lower[at] * (one / both) + upper[at] * (two / both)).astype(BF16))
    for h, result in enumerate(results):
        out[h * HD : (h + 1) * HD, :] = result
    if out.shape[0] > width:
        out[width:, :] = pack_levels(levels)


def combine(flip, own, other, rows, after=()):
    return call(
        combine_body, [struct((rows, own.shape[1]), BF16)], [flip], [own, other], after,
        blocked=True,
    )[0]


def attend_body(distances, last, mine, low, query, *refs):
    width, rows = query.shape
    half = rows // 2
    heads = width // HD
    blocks = refs[: len(distances)]
    state = refs[len(distances) :]
    accum, largest, total = refs[-3:]
    if distances[0] == 0:
        accum[...] = jnp.zeros(accum.shape, F32)
        largest[...] = jnp.full(largest.shape, FLOOR, F32)
        total[...] = jnp.zeros(total.shape, F32)
    else:
        accum[...] = state[0][...]
        largest[...] = state[1][...]
        total[...] = state[2][...]

    def visit(distance, block, i, until, j):
        q_at = slice(i * half, until * half)
        k_half = slice(j * half, (j + 1) * half)
        shape = (half, (until - i) * half)
        key_slot = (
            j * half - distance * rows + lax.broadcasted_iota(jnp.int32, shape, 0)
        )
        allowed = key_slot >= low[:, q_at]
        if distance == 0:
            query_slot = i * half + lax.broadcasted_iota(jnp.int32, shape, 1)
            allowed = allowed & (key_slot <= query_slot)
        scores = [
            mm_first(
                block[2 * h * HD : (2 * h + 1) * HD, k_half],
                query[h * HD : (h + 1) * HD, q_at],
            )
            for h in range(heads)
        ]
        parts = []
        for h in range(heads):
            score = jnp.where(allowed, scores[h] * (HD**-0.5 * LOG2_E), NEG)
            m_old = largest[h : h + 1, q_at]
            m_new = jnp.maximum(m_old, jnp.max(score, axis=0, keepdims=True))
            parts.append((m_new, jnp.exp2(score - m_new), jnp.exp2(m_old - m_new)))
        done = []
        for h, (m_new, weights, factor) in enumerate(parts):
            v_at = slice((2 * h + 1) * HD, (2 * h + 2) * HD)
            t_new = total[h : h + 1, q_at] * factor + jnp.sum(weights, axis=0, keepdims=True)
            mixed = accum[h * HD : (h + 1) * HD, q_at] * factor + mm(
                block[v_at, k_half], weights.astype(BF16)
            )
            done.append((m_new, t_new, mixed))
        for h, (m_new, t_new, mixed) in enumerate(done):
            accum[h * HD : (h + 1) * HD, q_at] = mixed
            largest[h : h + 1, q_at] = m_new
            total[h : h + 1, q_at] = t_new

    limits = [jnp.min(low[:, i * half : (i + 1) * half]) for i in range(2)]
    for distance, block in zip(distances, blocks):
        for j in range(2):
            end = (j + 1) * half - distance * rows
            if distance == 0 and j == 1:
                pl.when(limits[1] < end)(partial(visit, distance, block, 1, 2, j))
            else:
                pl.when(limits[1] < end)(partial(visit, distance, block, 0, 2, j))
                pl.when((limits[1] >= end) & (limits[0] < end))(
                    partial(visit, distance, block, 0, 1, j)
                )
    if last:
        out = refs[-4]
        for h in range(heads):
            at = slice(h * HD, (h + 1) * HD)
            t_h = total[h : h + 1, :]
            accum[at, :] = accum[at, :] * (1.0 / jnp.where(t_h > 0, t_h, 1.0))
        out[...] = accum[...].T.astype(BF16)


def attend(distances, last, mine, low, query, blocks, state, length=0, after=()):
    width, rows = query.shape
    shapes = [struct((width, rows), F32), struct((8, rows), F32), struct((8, rows), F32)]
    scratch = []
    outs = shapes
    if last:
        scratch = [pltpu.VMEM(s.shape, s.dtype) for s in shapes]
        outs = [struct((rows, width), BF16)]
    return call(
        partial(attend_body, distances, last),
        outs,
        [mine],
        [low, query, *blocks, *state],
        after,
        scratch,
        length,
        blocked=distances[0] > 0,
    )


def rows_body(gain_far, weight_far, *refs):
    parts, weights = refs[:4], refs[4:7]
    tokens = refs[7]
    squares, scaled, again, gain, own_weight, sems = refs[-6:]
    copies = [
        pltpu.make_async_copy(weight_far, own_weight, sems.at[0]),
        pltpu.make_async_copy(gain_far, gain, sems.at[1]),
    ]
    for copy in copies:
        copy.start()
    summed = sum(
        mm(w[...], a[...]).astype(BF16).astype(F32) for a, w in zip(parts[1:], weights)
    )
    copies[0].wait()
    summed = summed + mm(own_weight[...], parts[0][...]).astype(BF16).astype(F32)
    rows = tokens[...].astype(F32) + summed
    squares[...] = jnp.sum(rows * rows, axis=0, keepdims=True)
    copies[1].wait()
    scaled[...] = (rows * (gain[...] * SHRINK)).astype(BF16)
    again[...] = scaled[...]


def logits_body(limit, start, vocab, scaled, *refs):
    out = refs[-1]
    first = (start[0] + pl.program_id(0)) * out.shape[0]
    row = first + lax.broadcasted_iota(jnp.int32, out.shape, 0)
    out[...] = jnp.where(row < limit, mm(vocab[...], scaled[...]), NEG).astype(BF16)


def half_logits(start, vocab, scaled, after=()):
    limit, width = vocab.shape
    count = scaled.shape[1]
    tile = pl.cdiv(limit, 4 * 32) * 32
    return pl.pallas_call(
        partial(logits_body, limit),
        grid_spec=pltpu.PrefetchScalarGridSpec(
            num_scalar_prefetch=1,
            grid=(2,),
            in_specs=[
                pl.BlockSpec((tile, width), lambda i, start: (start[0] + i, 0)),
                pl.BlockSpec((width, count), lambda i, start: (0, 0)),
            ]
            + [ANYWHERE] * len(after),
            out_specs=pl.BlockSpec((tile, count), lambda i, start: (i, 0)),
        ),
        out_shape=struct((2 * tile, count), BF16),
        compiler_params=pltpu.CompilerParams(vmem_limit_bytes=VMEM_LIMIT),
        cost_estimate=pl.CostEstimate(flops=0, bytes_accessed=0, transcendentals=0),
    )(start, vocab, scaled, *after)


def fold_body(side, kept, came, send, keep):
    quarter = send.shape[0]
    for out, turn in ((send, 1 - side[0]), (keep, side[0])):
        at = pl.ds(pl.multiple_of(turn * quarter, 16), quarter)
        out[...] = (kept[at, :].astype(F32) + came[at, :].astype(F32)).astype(out.dtype)


def top_body(kept, came, *refs):
    out = refs[-1]
    out[...] = jnp.max(kept[...] + came[...].astype(F32), axis=0, keepdims=True)


def pair_body(first, second, *refs):
    refs[-1][0:1, :] = first[...]
    refs[-1][1:2, :] = second[...]


def split_columns(mine, source, outs):
    width = outs[0].shape[0]
    for b in range(4):
        at = pl.ds(pl.multiple_of((mine[0] ^ b) * width, width), width)
        outs[b][...] = source[:, at].T


def shards(
    tokens,
    norm_gain,
    w_query,
    w_key,
    w_value,
    w_out,
    final_gain,
    w_vocab,
    segment_ids,
    prompt_lengths,
    request_slots,
):
    rows, columns = tokens.shape
    half = rows // 2
    width = w_query.shape[1]
    heads = width // HD
    n_seq = lax.axis_size("seq")
    span = n_seq // 4
    seq_index = lax.axis_index("seq")
    tp_index = lax.axis_index("tp")
    mine = tp_index.reshape(1)
    base = seq_index * rows
    requests = request_slots.shape[0]

    powers = np.arange(HD // 2, dtype=np.float32) * np.float32(2.0 / HD)
    inverse = (np.float32(10000.0) ** -powers).astype(np.float32)[:, None]
    cosine, sine, low, request_low = call(
        prepare_body,
        [
            struct((HD // 2, rows), F32),
            struct((HD // 2, rows), F32),
            struct((1, rows), jnp.int32),
            struct((1, requests), jnp.int32),
        ],
        [base.reshape(1), prompt_lengths],
        [segment_ids[None, :], jnp.asarray(inverse)],
        blocked=True,
    )
    far = swap(tokens, "tp", 2)
    pieces = [tokens, swap(tokens, "tp", 1), far]
    gain = norm_gain.reshape(4, columns)
    weights = [
        pltpu.with_memory_space_constraint(w, pltpu.HBM) for w in (w_key, w_value, w_query)
    ]
    *sums, w_split, w_1, w_2, w_3, far_weights, last_kv, last_query = project(
        (0, 1), mine, gain, pieces[:2], weights, after=(cosine,), w_out=w_out
    )
    w_parts = [w_split] + [swap(w, "tp", b) for b, w in ((1, w_1), (2, w_2), (3, w_3))]
    (relayed,) = call(copy_body, [struct(far.shape, BF16)], [], [far], sums[1:])
    pieces.append(swap(relayed, "tp", 1))

    asked = request_slots[None, :]
    inside = asked - base
    (own_tokens,) = call(
        pick_body, [struct((columns, requests), BF16)], [base.reshape(1)], [asked, tokens],
        blocked=True,
    )
    all_tokens = [own_tokens]
    last_gain = final_gain[:, None]
    *kv_sums, query_sums, query_squares = project(
        (2,), mine, gain, pieces[2:3], [far_weights], sums, None, (last_gain,), length=10
    )
    ending = (base.reshape(1), cosine, sine, asked)
    query, own_query = project(
        (3,), mine, gain, pieces[3:], [last_query], (query_sums, query_squares), ending, (), 2, (2,)
    )
    asking = [own_query] + [shifted(own_query, "seq", -by) for by in range(1, span + 1)]
    bit = n_seq // 2
    while bit:
        all_tokens += call(
            add_body,
            [struct(own_tokens.shape, BF16)],
            [],
            [all_tokens[-1], swap(all_tokens[-1], "seq", bit)],
            sums[1:2] if len(all_tokens) == 1 else (own_query,),
        )
        bit //= 2
    (kv,) = project(
        (3,),
        mine,
        gain,
        pieces[3:],
        [last_kv],
        kv_sums,
        ending,
        (own_query,),
        10,
        (0, 1),
    )

    kv_cache = jnp.transpose(kv.reshape(heads, 2 * HD, rows), (0, 2, 1))
    behind = shifted(kv, "seq", 1)

    (mixed,) = call(
        partial(request_body, len(asking)),
        [struct((width + LEVEL_ROWS, requests), BF16)],
        [],
        [request_low, inside, kv, *asking],
        all_tokens[3:4],
    )
    own_state = attend((0,), False, mine, low, query, (kv,), (), length=10, after=(mixed,))

    afters = [own_state[1:2], all_tokens[-1:] if n_seq > 8 else (), w_parts[2:3]]
    stages = [mixed]
    bit = 1
    while bit < n_seq:
        flip = ((seq_index & bit) > 0).astype(jnp.int32).reshape(1)
        after = afters.pop(0) if afters else ()
        bit *= 2
        kept_rows = width + LEVEL_ROWS if bit < n_seq else width
        other = swap(stages[-1], "seq", bit // 2)
        stages.append(combine(flip, stages[-1], other, kept_rows, after))
    request_mixed = spread(stages[-1])
    (later_kv,) = call(copy_body, [struct(kv.shape, BF16)], [], [kv], stages[-1:])

    core = tp_index & 1
    side = tp_index >> 1
    squares, scaled, again = call(
        rows_body,
        [struct((1, requests), F32)] + [struct(own_tokens.shape, BF16)] * 2,
        [],
        [*request_mixed, *w_parts[1:], all_tokens[-1]],
        scratch=[
            pltpu.VMEM((columns, 1), F32),
            pltpu.VMEM((columns, width), BF16),
            pltpu.SemaphoreType.DMA((2,)),
        ],
        far=pinned([last_gain, w_split]),
    )
    vocab = pltpu.with_memory_space_constraint(w_vocab.T, pltpu.HBM)
    sent = half_logits((2 * (1 - core)).reshape(1), vocab, scaled)
    kept = half_logits((2 * core).reshape(1), vocab, again, (sent,))
    quarter = kept.shape[0] // 2
    sent, kept = call(
        fold_body,
        [struct((quarter, requests), BF16), struct((quarter, requests), F32)],
        [side.reshape(1)],
        [kept, swap(sent, "tp", 1)],
    )
    blocks = [behind] + [shifted(later_kv, "seq", by) for by in range(2, span + 1)]
    distances = list(range(1, span + 1))
    state = own_state
    while distances:
        last = len(distances) <= 3
        state = attend(distances[:3], last, mine, low, query, blocks[:3], state, 30)
        distances, blocks = distances[3:], blocks[3:]
    (best,) = call(
        top_body, [struct((1, requests), F32)], [], [kept, swap(sent, "tp", 2)], state[:1]
    )
    bit = 1
    while bit < n_seq:
        best = jnp.maximum(best, swap(best, "seq", bit))
        bit *= 2
    attended = spread(state[0])
    (pair,) = call(
        pair_body, [struct((2, requests), F32)], [], [best, squares], attended[2:3]
    )
    for bit in (2, 1):
        other = swap(pair, "tp", bit)
        pair = jnp.stack([jnp.maximum(pair[0], other[0]), pair[1] + other[1]])
    hidden_norm = jnp.sqrt(pair[1] / D + EPS)
    top_logit = pair[0] / hidden_norm * (1.0 / SHRINK)

    summed = sum(
        mm_last(part, w).astype(BF16).astype(F32) for part, w in zip(attended, w_parts)
    )
    hidden = (tokens.astype(F32) + summed).astype(BF16)
    return (kv_cache, hidden, hidden_norm, top_logit)


def solution(mesh):
    return jax.shard_map(
        shards,
        mesh=mesh,
        in_specs=(
            P("seq", "tp"),
            P(),
            P(None, "tp"),
            P(None, "tp"),
            P(None, "tp"),
            P("tp", None),
            P("tp"),
            P("tp", "seq"),
            P("seq"),
            P(),
            P(),
        ),
        out_specs=(P("tp", "seq", None), P("seq", "tp"), P(), P()),
        check_vma=False,
    )
```

```python
from functools import partial

import jax
import jax.numpy as jnp
import numpy as np
from jax import lax
from jax.experimental import pallas as pl
from jax.experimental.pallas import tpu as pltpu
from jax.sharding import PartitionSpec as P

D = 3072
HD = 96
EPS = 1e-05
NEG = -1e30
FLOOR = -5e29
NEVER = 2**30
LEVEL_ROWS = 16
SHRINK = 2.0**-16
DAMP = 2.0**-24
LOG2_E = 1.4426950408889634
F32 = jnp.float32
BF16 = jnp.bfloat16
VMEM_LIMIT = 12 * 1024 * 1024

SCALARS = pl.BlockSpec(memory_space=pltpu.SMEM)
ANYWHERE = pl.BlockSpec(memory_space=pl.ANY)
FAR_MEMORY = pl.BlockSpec(memory_space=pltpu.HBM)


WHOLE = pl.BlockSpec(memory_space=pltpu.VMEM)


def whole(array):
    return pl.BlockSpec(array.shape, lambda i: (0, 0), pipeline_mode=pl.Buffered(1))


def call(body, outs, scalars, arrays, after=(), scratch=(), length=0, far=(), blocked=False):
    return pl.pallas_call(
        body,
        grid=(1,) if blocked else (),
        out_shape=outs,
        in_specs=[SCALARS] * len(scalars)
        + [FAR_MEMORY] * len(far)
        + [whole(array) if blocked else WHOLE for array in arrays]
        + [ANYWHERE] * len(after),
        out_specs=[whole(out) if blocked else WHOLE for out in outs],
        scratch_shapes=list(scratch),
        compiler_params=pltpu.CompilerParams(vmem_limit_bytes=VMEM_LIMIT),
        cost_estimate=pl.CostEstimate(
            flops=length * 10**9, bytes_accessed=0, transcendentals=0
        ),
    )(*scalars, *far, *arrays, *after)


def pinned(arrays):
    return [pltpu.with_memory_space_constraint(a, pltpu.HBM) for a in arrays]


def struct(shape, dtype):
    return jax.ShapeDtypeStruct(shape, dtype)


def swap(array, axis, bit):
    count = lax.axis_size(axis)
    return lax.ppermute(array, axis, [(i, i ^ bit) for i in range(count)])


def shifted(array, axis, by):
    count = lax.axis_size(axis)
    pairs = [(i, i + by) for i in range(count) if 0 <= i + by < count]
    return lax.ppermute(array, axis, pairs)


def spread(array):
    far = swap(array, "tp", 2)
    near = swap(array, "tp", 1)
    return array, near, far, swap(far, "tp", 1)


def mm(a, b):
    return jnp.dot(a, b, preferred_element_type=F32)


def mm_last(a, b):
    return lax.dot_general(a, b, (((1,), (1,)), ((), ())), preferred_element_type=F32)


def mm_first(a, b):
    return lax.dot_general(a, b, (((0,), (0,)), ((), ())), preferred_element_type=F32)


AHEAD = ((2, (0, 1, 2)), (3, (0, 1)), (3, (2,)))


def project_body(blocks, first, last, kinds, *refs):
    refs = list(refs)
    take = lambda count: [refs.pop(0) for _ in range(count)]
    mine = refs.pop(0)
    base = refs.pop(0) if last else None
    weights = take(3 if first else 1)
    (gain,) = take(1)
    pieces = take(len(blocks))
    accum, squares = take(2) if not first else (None, None)
    cosine, sine, asked = take(3) if last else (None, None, None)
    if first:
        held, sems = refs[-2:]
        del refs[-2:]
    rows, part = pieces[0].shape
    width = weights[0].shape[-1]
    copies = []
    onward = []
    if first:
        split_columns(mine, refs.pop(0), refs[-7:-3])
        for (block, needed), out in zip(AHEAD, refs[-3:]):
            at = pl.ds(pl.multiple_of((mine[0] ^ block) * part, part), part)
            onward += [
                pltpu.make_async_copy(weights[i].at[at, :], out.at[j], sems.at[i, block])
                for j, i in enumerate(needed)
            ]
        del refs[-7:]
    for i in range(3 if first else 0):
        for j, block in enumerate(blocks):
            at = pl.ds(pl.multiple_of((mine[0] ^ block) * part, part), part)
            copies.append(
                pltpu.make_async_copy(weights[i].at[at, :], held.at[i, j], sems.at[i, j])
            )
    for copy in copies + onward:
        copy.start()
    wide = [piece[...].astype(F32) for piece in pieces]
    total = sum(jnp.sum(w * w, axis=1, keepdims=True) for w in wide)
    if not first:
        total = total + squares[...]
    scaled = [
        (w * (gain[pl.ds(mine[0] ^ block, 1), :] * DAMP)).astype(BF16)
        for block, w in zip(blocks, wide)
    ]
    factor = lax.rsqrt(total / D + EPS) * (1.0 / DAMP)
    middle = HD // 2
    for i in kinds:
        place = kinds.index(i)
        at = slice(place * width, (place + 1) * width)
        field = 0.0
        for j, x in enumerate(scaled):
            if first:
                copies[i * len(blocks) + j].wait()
                field = field + mm(x, held[i, j])
            else:
                field = field + mm(x, weights[0][place])
        if not first:
            field = field + accum[:, at]
        if first:
            refs[-2][:, at] = field
            continue
        if not last:
            out = refs[-4] if i < 2 else refs[-2]
            out[:, at if i < 2 else slice(0, width)] = field
            continue
        field = (field * factor).T
        if 2 in kinds:
            query, own = refs[-2:]
        else:
            kv = refs[-4]
        for h in range(width // HD):
            at = h * HD
            a = field[at : at + middle]
            b = field[at + middle : at + HD]
            if i == 1:
                kv[2 * at + HD : 2 * at + 2 * HD, :] = field[at : at + HD].astype(BF16)
            else:
                to, out = (at, query) if i == 2 else (2 * at, kv)
                out[to : to + middle, :] = (a * cosine[...] - b * sine[...]).astype(BF16)
                out[to + middle : to + HD, :] = (b * cosine[...] + a * sine[...]).astype(BF16)
    if last and 2 not in kinds:
        refs[-3][...] = kv[...]
        refs[-2][...] = kv[...]
        refs[-1][...] = kv[:, rows // 2 :]
    if last and 2 in kinds:
        row = base[0] + lax.broadcasted_iota(jnp.int32, (rows, asked.shape[1]), 0)
        own[...] = mm(query[...], (asked[...] == row).astype(BF16)).astype(BF16)
    if not last:
        refs[-1][...] = total
        if not first:
            refs[-3][...] = total
    for copy in onward:
        copy.wait()


def project(
    blocks,
    mine,
    gain,
    pieces,
    weights,
    before=(),
    ending=None,
    after=(),
    length=0,
    kinds=(0, 1, 2),
    w_out=None,
):
    rows = pieces[0].shape[0]
    width = weights[0].shape[-1]
    scalars, arrays = [mine], [gain, *pieces, *before]
    if ending is None:
        outs = [struct((rows, 3 * width), F32), struct((rows, 1), F32)]
        if before:
            outs = [struct((rows, 2 * width), F32), struct((rows, 1), F32)]
            outs += [struct((rows, width), F32), struct((rows, 1), F32)]
    if not before:
        arrays.append(w_out)
        outs += [struct((w_out.shape[1] // 4, w_out.shape[0]), BF16)] * 4
        outs += [struct((len(n), pieces[0].shape[1], width), BF16) for _, n in AHEAD]
    if ending is not None:
        base, cosine, sine, asked = ending
        scalars.append(base)
        arrays += [cosine, sine, asked]
        outs = [struct((2 * width, rows), BF16)] * 3 + [struct((2 * width, rows // 2), BF16)]
        if 2 in kinds:
            outs = [struct((width, rows), BF16), struct((width, asked.shape[1]), BF16)]
    body = partial(project_body, blocks, not before, ending is not None, kinds)
    if before:
        arrays = list(weights) + arrays
        return call(body, outs, scalars, arrays, after, length=length)
    scratch = [
        pltpu.VMEM((3, len(blocks), pieces[0].shape[1], width), BF16),
        pltpu.SemaphoreType.DMA((3, 4)),
    ]
    return call(body, outs, scalars, arrays, after, scratch, length, weights)


def copy_body(source, *refs):
    refs[-1][...] = source[...]


def twice_body(source, *refs):
    refs[-2][...] = source[...]
    refs[-1][...] = source[...]


def prepare_body(base, lengths, segments, inverse, *refs):
    cosine, sine, low, asked_low = refs[-4:]
    prompts = lengths.shape[0]
    rows = segments.shape[1]
    segment = segments[...]
    asked = lax.broadcasted_iota(jnp.int32, asked_low.shape, 1)
    each = asked_low.shape[1] // prompts
    first = jnp.zeros((1, rows), jnp.int32)
    asked_first = jnp.zeros(asked_low.shape, jnp.int32)
    start = jnp.int32(0)
    for p in range(prompts):
        first = jnp.where(segment == p, start, first)
        asked_first = jnp.where(
            (asked >= p * each) & (asked < (p + 1) * each), start, asked_first
        )
        start = start + lengths[p]
    valid = segment >= 0
    slot = base[0] + lax.broadcasted_iota(jnp.int32, (1, rows), 1)
    position = jnp.where(valid, slot - first, 0).astype(F32)
    angles = inverse[...] * position
    cosine[...] = jnp.cos(angles)
    sine[...] = jnp.sin(angles)
    low[...] = jnp.where(valid, first - base[0], NEVER)
    asked_low[...] = asked_first - base[0]


def pick_body(base, slots, tokens, out):
    rows = tokens.shape[0]
    count = slots.shape[1]
    row = base[0] + lax.broadcasted_iota(jnp.int32, (rows, count), 0)
    out[...] = mm_first(tokens[...], (slots[...] == row).astype(BF16)).astype(BF16)


def add_body(first, second, *refs):
    refs[-1][...] = first[...] + second[...]


def request_body(count, low, high, block, *refs):
    query = sum(part[...] for part in refs[:count])
    width, rows = query.shape
    half = block.shape[1] // 2
    allowed = []
    for i in range(2):
        key_slot = i * half + lax.broadcasted_iota(jnp.int32, (half, rows), 0)
        allowed.append((key_slot >= low[...]) & (key_slot <= high[...]))
    results = []
    levels = []
    for h in range(width // HD):
        at = slice(h * HD, (h + 1) * HD)
        k_at = slice(2 * h * HD, (2 * h + 1) * HD)
        v_at = slice((2 * h + 1) * HD, (2 * h + 2) * HD)
        scores = [
            jnp.where(
                allowed[i], mm_first(block[k_at, i * half : (i + 1) * half], query[at, :]) * HD**-0.5, NEG
            )
            for i in range(2)
        ]
        largest = jnp.maximum(*[jnp.max(part, axis=0, keepdims=True) for part in scores])
        largest = jnp.maximum(largest, FLOOR)
        weights = [jnp.exp(part - largest) for part in scores]
        total = sum(jnp.sum(part, axis=0, keepdims=True) for part in weights)
        mixed = sum(
            mm(block[v_at, i * half : (i + 1) * half], weights[i].astype(BF16)) for i in range(2)
        )
        filled = total > 0
        safe = jnp.where(filled, total, 1.0)
        results.append((mixed * (1.0 / safe)).astype(BF16))
        levels.append(jnp.where(filled, largest + jnp.log(safe), NEG))
    out = refs[-1]
    for h, result in enumerate(results):
        out[h * HD : (h + 1) * HD, :] = result
    out[width:, :] = pack_levels(levels)


def pack_levels(levels):
    row = lax.broadcasted_iota(jnp.int32, (LEVEL_ROWS, levels[0].shape[1]), 0)
    packed = jnp.zeros(row.shape, F32)
    for h, level in enumerate(levels):
        for part in range(3):
            rounded = level.astype(BF16).astype(F32)
            packed = jnp.where(row == 3 * h + part, rounded, packed)
            level = level - rounded
    return packed.astype(BF16)


def combine_body(flip, own, other, *refs):
    width = own.shape[0] - LEVEL_ROWS
    turned = flip[0] > 0
    a = own[...].astype(F32)
    b = other[...].astype(F32)
    lower = jnp.where(turned, b, a)
    upper = jnp.where(turned, a, b)
    levels = []
    results = []
    for h in range(width // HD):
        marks = []
        for side in (lower, upper):
            at = width + 3 * h
            marks.append(side[at : at + 1] + side[at + 1 : at + 2] + side[at + 2 : at + 3])
        top = jnp.maximum(*marks)
        one, two = (jnp.exp(mark - top) for mark in marks)
        both = one + two
        levels.append(top + jnp.log(both))
        at = slice(h * HD, (h + 1) * HD)
        results.append((lower[at] * (one / both) + upper[at] * (two / both)).astype(BF16))
    out = refs[-1]
    for h, result in enumerate(results):
        out[h * HD : (h + 1) * HD, :] = result
    if out.shape[0] > width:
        out[width:, :] = pack_levels(levels)


def combine(flip, own, other, rows, after=()):
    return call(
        combine_body,
        [struct((rows, own.shape[1]), BF16)],
        [flip],
        [own, other],
        after,
        blocked=True,
    )[0]


def attend_body(sources, last, place, low, query, *refs):
    width, rows = query.shape
    half = rows // 2
    heads = width // HD
    blocks = refs[: len(sources)]
    state = refs[len(sources) :]
    accum, largest, total = refs[-3:]
    if sources[0][0] == 0:
        accum[...] = jnp.zeros(accum.shape, F32)
        largest[...] = jnp.full(largest.shape, FLOOR, F32)
        total[...] = jnp.zeros(total.shape, F32)
    else:
        accum[...] = state[0][...]
        largest[...] = state[1][...]
        total[...] = state[2][...]

    def visit(distance, block, part, i, until, j):
        q_at = slice(i * half, until * half)
        k_half = slice(part * half, (part + 1) * half)
        shape = (half, (until - i) * half)
        key_slot = (
            j * half - distance * rows + lax.broadcasted_iota(jnp.int32, shape, 0)
        )
        allowed = key_slot >= low[:, q_at]
        if distance == 0:
            query_slot = i * half + lax.broadcasted_iota(jnp.int32, shape, 1)
            allowed = allowed & (key_slot <= query_slot)
        scores = [
            mm_first(
                block[2 * h * HD : (2 * h + 1) * HD, k_half],
                query[h * HD : (h + 1) * HD, q_at],
            )
            for h in range(heads)
        ]
        parts = []
        for h in range(heads):
            score = jnp.where(allowed, scores[h] * (HD**-0.5 * LOG2_E), NEG)
            m_old = largest[h : h + 1, q_at]
            m_new = jnp.maximum(m_old, jnp.max(score, axis=0, keepdims=True))
            parts.append((m_new, jnp.exp2(score - m_new), jnp.exp2(m_old - m_new)))
        done = []
        for h, (m_new, weights, factor) in enumerate(parts):
            v_at = slice((2 * h + 1) * HD, (2 * h + 2) * HD)
            t_new = total[h : h + 1, q_at] * factor + jnp.sum(weights, axis=0, keepdims=True)
            mixed = accum[h * HD : (h + 1) * HD, q_at] * factor + mm(
                block[v_at, k_half], weights.astype(BF16)
            )
            done.append((m_new, t_new, mixed))
        for h, (m_new, t_new, mixed) in enumerate(done):
            accum[h * HD : (h + 1) * HD, q_at] = mixed
            largest[h : h + 1, q_at] = m_new
            total[h : h + 1, q_at] = t_new

    limits = [jnp.min(low[:, i * half : (i + 1) * half]) for i in range(2)]
    for (distance, least, most, skipped), block in zip(sources, blocks):
        here = (place[0] >= least) & (place[0] <= most)
        for j in range(skipped, 2):
            end = (j + 1) * half - distance * rows
            look = partial(visit, distance, block, j - skipped)
            if distance == 0 and j == 1:
                pl.when(limits[1] < end)(partial(look, 1, 2, j))
            else:
                pl.when(here & (limits[1] < end))(partial(look, 0, 2, j))
                pl.when(here & (limits[1] >= end) & (limits[0] < end))(partial(look, 0, 1, j))
    if last:
        out = refs[-4]
        for h in range(heads):
            at = slice(h * HD, (h + 1) * HD)
            t_h = total[h : h + 1, :]
            accum[at, :] = accum[at, :] * (1.0 / jnp.where(t_h > 0, t_h, 1.0))
        out[...] = accum[...].T.astype(BF16)


def attend(sources, last, place, low, query, blocks, state, length=0, after=()):
    width, rows = query.shape
    shapes = [struct((width, rows), F32), struct((8, rows), F32), struct((8, rows), F32)]
    scratch = []
    outs = shapes
    if last:
        scratch = [pltpu.VMEM(s.shape, s.dtype) for s in shapes]
        outs = [struct((rows, width), BF16)]
    return call(
        partial(attend_body, sources, last),
        outs,
        [place],
        [low, query, *blocks, *state],
        after,
        scratch,
        length,
        blocked=True,
    )


def begin_body(limit, start, vocab, weight_far, tail, tokens, own, near, near_weight, *refs):
    half, base, weight, sems = refs[-4:]
    rows = half.shape[0]
    whole_rows = (limit - rows) // 16 * 16
    lower = start[0] == 0

    def fetch(at, count):
        return pltpu.make_async_copy(
            vocab.at[pl.ds(at, count), :], half.at[pl.ds(0, count), :], sems.at[0]
        )

    load = pltpu.make_async_copy(weight_far, weight, sems.at[1])
    load.start()

    @pl.when(lower)
    def _():
        fetch(0, rows).start()

    @pl.when(jnp.logical_not(lower))
    def _():
        fetch(rows, whole_rows).start()

    field = tokens[...].astype(F32) + mm(near_weight[...], near[...]).astype(BF16).astype(F32)
    load.wait()
    base[...] = field + mm(weight[...], own[...]).astype(BF16).astype(F32)

    @pl.when(lower)
    def _():
        fetch(0, rows).wait()

    @pl.when(jnp.logical_not(lower))
    def _():
        fetch(rows, whole_rows).wait()
        if limit > rows + whole_rows:
            half[whole_rows : whole_rows + 16, :] = tail[...]


def begin_rows(start, vocab, weight_far, tokens, own, near, near_weight):
    limit, width = vocab.shape
    count = tokens.shape[1]
    rows = pl.cdiv(limit, 4 * 32) * 64
    last_tile = (limit - 1) // 16
    return pl.pallas_call(
        partial(begin_body, limit),
        grid=(1,),
        out_shape=[struct((rows, width), BF16), struct((width, count), F32)],
        in_specs=[SCALARS, FAR_MEMORY, FAR_MEMORY]
        + [pl.BlockSpec((16, width), lambda i: (last_tile, 0))]
        + [whole(a) for a in (tokens, own, near, near_weight)],
        out_specs=[WHOLE, whole(tokens)],
        scratch_shapes=[pltpu.VMEM(weight_far.shape, BF16), pltpu.SemaphoreType.DMA((2,))],
        compiler_params=pltpu.CompilerParams(vmem_limit_bytes=VMEM_LIMIT),
        cost_estimate=pl.CostEstimate(flops=3 * 10**9, bytes_accessed=0, transcendentals=0),
    )(start, vocab, weight_far, vocab, tokens, own, near, near_weight)


def rows_body(gain_far, base, far, last, far_weight, last_weight, *refs):
    squares, scaled, again, gain, sem = refs[-5:]
    copy = pltpu.make_async_copy(gain_far, gain, sem.at[0])
    copy.start()
    rows = base[...] + mm(far_weight[...], far[...]).astype(BF16).astype(F32)
    rows = rows + mm(last_weight[...], last[...]).astype(BF16).astype(F32)
    squares[...] = jnp.sum(rows * rows, axis=0, keepdims=True)
    copy.wait()
    scaled[...] = (rows * (gain[...] * SHRINK)).astype(BF16)
    again[...] = scaled[...]


def held_body(limit, start, half, scaled, out):
    row = start[0] + lax.broadcasted_iota(jnp.int32, out.shape, 0)
    out[...] = jnp.where(row < limit, mm(half[...], scaled[...]), NEG).astype(BF16)


def logits_body(limit, start, vocab, scaled, *refs):
    out = refs[-1]
    first = (start[0] + pl.program_id(0)) * out.shape[0]
    row = first + lax.broadcasted_iota(jnp.int32, out.shape, 0)
    out[...] = jnp.where(row < limit, mm(vocab[...], scaled[...]), NEG).astype(BF16)


def half_logits(start, vocab, scaled, after=()):
    limit, width = vocab.shape
    count = scaled.shape[1]
    tile = pl.cdiv(limit, 4 * 32) * 32
    return pl.pallas_call(
        partial(logits_body, limit),
        grid_spec=pltpu.PrefetchScalarGridSpec(
            num_scalar_prefetch=1,
            grid=(2,),
            in_specs=[
                pl.BlockSpec((tile, width), lambda i, start: (start[0] + i, 0)),
                pl.BlockSpec((width, count), lambda i, start: (0, 0)),
            ]
            + [ANYWHERE] * len(after),
            out_specs=pl.BlockSpec((tile, count), lambda i, start: (i, 0)),
        ),
        out_shape=struct((2 * tile, count), BF16),
        compiler_params=pltpu.CompilerParams(vmem_limit_bytes=VMEM_LIMIT),
        cost_estimate=pl.CostEstimate(flops=0, bytes_accessed=0, transcendentals=0),
    )(start, vocab, scaled, *after)


def fold_body(side, kept, came, send, keep):
    quarter = send.shape[0]
    for out, turn in ((send, 1 - side[0]), (keep, side[0])):
        at = pl.ds(pl.multiple_of(turn * quarter, 16), quarter)
        out[...] = (kept[at, :].astype(F32) + came[at, :].astype(F32)).astype(out.dtype)


def top_body(kept, came, *refs):
    out = refs[-1]
    out[...] = jnp.max(kept[...] + came[...].astype(F32), axis=0, keepdims=True)


def pair_body(first, second, *refs):
    refs[-1][0:1, :] = first[...]
    refs[-1][1:2, :] = second[...]


def split_columns(mine, source, outs):
    width = outs[0].shape[0]
    for b in range(4):
        at = pl.ds(pl.multiple_of((mine[0] ^ b) * width, width), width)
        outs[b][...] = source[:, at].T


def shards(
    tokens,
    norm_gain,
    w_query,
    w_key,
    w_value,
    w_out,
    final_gain,
    w_vocab,
    segment_ids,
    prompt_lengths,
    request_slots,
):
    rows, columns = tokens.shape
    half = rows // 2
    width = w_query.shape[1]
    heads = width // HD
    n_seq = lax.axis_size("seq")
    span = n_seq // 4
    seq_index = lax.axis_index("seq")
    tp_index = lax.axis_index("tp")
    mine = tp_index.reshape(1)
    base = seq_index * rows
    requests = request_slots.shape[0]
    prompts = prompt_lengths.shape[0]

    far = swap(tokens, "tp", 2)
    pieces = [tokens, swap(tokens, "tp", 1), far]
    gain = norm_gain.reshape(4, columns)
    weights = [
        pltpu.with_memory_space_constraint(w, pltpu.HBM) for w in (w_key, w_value, w_query)
    ]
    *sums, w_split, w_1, w_2, w_3, far_weights, last_kv, last_query = project(
        (0, 1), mine, gain, pieces[:2], weights, w_out=w_out
    )
    w_parts = [w_split] + [swap(w, "tp", b) for b, w in ((1, w_1), (2, w_2), (3, w_3))]
    powers = np.arange(HD // 2, dtype=np.float32) * np.float32(2.0 / HD)
    inverse = (np.float32(10000.0) ** -powers).astype(np.float32)[:, None]
    cosine, sine, low, request_low = call(
        prepare_body,
        [
            struct((HD // 2, rows), F32),
            struct((HD // 2, rows), F32),
            struct((1, rows), jnp.int32),
            struct((1, requests), jnp.int32),
        ],
        [base.reshape(1), prompt_lengths],
        pinned([segment_ids[None, :], jnp.asarray(inverse)]),
        sums[1:2],
        blocked=True,
    )
    last_gain = final_gain[:, None]
    relayed, far = call(
        twice_body, [struct(far.shape, BF16)] * 2, [], [far], (sums[1], cosine, last_gain)
    )
    pieces = pieces[:2] + [far, swap(relayed, "tp", 1)]

    asked = request_slots[None, :]
    inside = asked - base
    (own_tokens,) = call(
        pick_body, [struct((columns, requests), BF16)], [base.reshape(1)], pinned([asked, tokens]),
        blocked=True,
    )
    all_tokens = [own_tokens]
    *kv_sums, query_sums, query_squares = project(
        (2,), mine, gain, pieces[2:3], [far_weights], sums, None, (), length=10
    )
    ending = (base.reshape(1), cosine, sine, asked)
    query, own_query = project(
        (3,), mine, gain, pieces[3:], [last_query], (query_sums, query_squares), ending, (), 2, (2,)
    )
    asking = [own_query] + [shifted(own_query, "seq", -by) for by in range(1, span + 1)]
    bit = n_seq // 2
    while bit:
        all_tokens += call(
            add_body,
            [struct(own_tokens.shape, BF16)],
            [],
            [all_tokens[-1], swap(all_tokens[-1], "seq", bit)],
            sums[1:2] if len(all_tokens) == 1 else (own_query,),
        )
        bit //= 2
    asked_kv, own_kv, kv, kv_half = project(
        (3,),
        mine,
        gain,
        pieces[3:],
        [last_kv],
        kv_sums,
        ending,
        (own_query,),
        10,
        (0, 1),
    )

    kv_cache = jnp.transpose(kv.reshape(heads, 2 * HD, rows), (0, 2, 1))
    behind = shifted(kv, "seq", 1)

    last_start = n_seq - span - 1
    ends = jnp.cumsum(prompt_lengths)
    reach = (ends - 1) // rows - (ends - prompt_lengths) // rows
    longest = jnp.max(jnp.where(jnp.arange(prompts) < prompts - 1, reach, 0))
    sources = [(0, 0, n_seq, 0), (1, 0, n_seq, 0)]
    blocks = [own_kv, behind]
    for by in range(2, span + 1):
        early = [(i, i + by) for i in range(last_start + 1 - by)]
        late = [(i, i + by) for i in range(last_start, n_seq - by)]
        sources.append((by, 0, last_start, 0))
        blocks.append(
            lax.cond(
                longest >= by,
                lambda array, pairs=early: lax.ppermute(array, "seq", pairs),
                jnp.zeros_like,
                kv,
            )
        )
        from_half = 1 if by == span else 0
        sources.append((by, last_start + by, n_seq, from_half))
        blocks.append(lax.ppermute(kv_half if from_half else kv, "seq", late))
    halo = tuple(blocks[2:4])

    (mixed,) = call(
        partial(request_body, len(asking)),
        [struct((width + LEVEL_ROWS, requests), BF16)],
        [],
        [request_low, inside, asked_kv, *asking],
        all_tokens[2:3],
    )
    afters = [all_tokens[3:4], (), w_parts[2:3] + [all_tokens[-1]]]
    bit = 1
    while bit < n_seq:
        flip = ((seq_index & bit) > 0).astype(jnp.int32).reshape(1)
        after = afters.pop(0) if afters else ()
        other = swap(mixed, "seq", bit)
        bit *= 2
        kept_rows = width + LEVEL_ROWS if bit < n_seq else width
        mixed = combine(flip, mixed, other, kept_rows, after)
    _, near_mixed, far_mixed, last_mixed = spread(mixed)

    core = tp_index & 1
    side = tp_index >> 1
    vocab = pltpu.with_memory_space_constraint(w_vocab.T, pltpu.HBM)
    limit = vocab.shape[0]
    vocab_rows = pl.cdiv(limit, 4 * 32) * 64
    away = (vocab_rows * (1 - core)).reshape(1)
    far_gain, own_weight = pinned([last_gain, w_split])
    held, field = begin_rows(
        away, vocab, own_weight, all_tokens[-1], mixed, near_mixed, w_parts[1]
    )
    squares, scaled, again = call(
        rows_body,
        [struct((1, requests), F32)] + [struct(own_tokens.shape, BF16)] * 2,
        [],
        [field, far_mixed, last_mixed, *w_parts[2:]],
        scratch=[pltpu.VMEM((columns, 1), F32), pltpu.SemaphoreType.DMA((1,))],
        far=[far_gain],
        after=halo[1:],
    )
    (sent,) = call(
        partial(held_body, limit),
        [struct((vocab_rows, requests), BF16)],
        [away],
        [held, scaled],
    )
    kept = half_logits((2 * core).reshape(1), vocab, again, (sent,))
    quarter = kept.shape[0] // 2
    sent, kept = call(
        fold_body,
        [struct((quarter, requests), BF16), struct((quarter, requests), F32)],
        [side.reshape(1)],
        [kept, swap(sent, "tp", 1)],
    )
    state = ()
    while sources:
        last = len(sources) <= 4
        state = attend(
            sources[:4], last, seq_index.reshape(1), low, query, blocks[:4], state, 30
        )
        sources, blocks = sources[4:], blocks[4:]
    (best,) = call(
        top_body, [struct((1, requests), F32)], [], [kept, swap(sent, "tp", 2)], state[:1]
    )
    bit = 1
    while bit < n_seq:
        best = jnp.maximum(best, swap(best, "seq", bit))
        bit *= 2
    attended = spread(state[0])
    (pair,) = call(
        pair_body, [struct((2, requests), F32)], [], [best, squares], attended[2:3]
    )
    for bit in (2, 1):
        other = swap(pair, "tp", bit)
        pair = jnp.stack([jnp.maximum(pair[0], other[0]), pair[1] + other[1]])
    hidden_norm = jnp.sqrt(pair[1] / D + EPS)
    top_logit = pair[0] / hidden_norm * (1.0 / SHRINK)

    summed = sum(
        mm_last(part, w).astype(BF16).astype(F32) for part, w in zip(attended, w_parts)
    )
    hidden = (tokens.astype(F32) + summed).astype(BF16)
    return (kv_cache, hidden, hidden_norm, top_logit)


def solution(mesh):
    return jax.shard_map(
        shards,
        mesh=mesh,
        in_specs=(
            P("seq", "tp"),
            P(),
            P(None, "tp"),
            P(None, "tp"),
            P(None, "tp"),
            P("tp", None),
            P("tp"),
            P("tp", "seq"),
            P("seq"),
            P(),
            P(),
        ),
        out_specs=(P("tp", "seq", None), P("seq", "tp"), P(), P()),
        check_vma=False,
    )
```

```python
from functools import partial

import jax
import jax.numpy as jnp
import numpy as np
from jax import lax
from jax.experimental import pallas as pl
from jax.experimental.pallas import tpu as pltpu
from jax.sharding import PartitionSpec as P

D = 3072
HD = 96
EPS = 1e-05
NEG = -1e30
FLOOR = -5e29
NEVER = 2**30
LEVEL_ROWS = 16
SHRINK = 2.0**-16
DAMP = 2.0**-24
LOG2_E = 1.4426950408889634
F32 = jnp.float32
BF16 = jnp.bfloat16
VMEM_LIMIT = 12 * 1024 * 1024

SCALARS = pl.BlockSpec(memory_space=pltpu.SMEM)
ANYWHERE = pl.BlockSpec(memory_space=pl.ANY)
FAR_MEMORY = pl.BlockSpec(memory_space=pltpu.HBM)


WHOLE = pl.BlockSpec(memory_space=pltpu.VMEM)


def whole(array):
    return pl.BlockSpec(array.shape, lambda i: (0, 0), pipeline_mode=pl.Buffered(1))


def call(body, outs, scalars, arrays, after=(), scratch=(), length=0, far=(), blocked=False):
    return pl.pallas_call(
        body,
        grid=(1,) if blocked else (),
        out_shape=outs,
        in_specs=[SCALARS] * len(scalars)
        + [FAR_MEMORY] * len(far)
        + [whole(array) if blocked else WHOLE for array in arrays]
        + [ANYWHERE] * len(after),
        out_specs=[whole(out) if blocked else WHOLE for out in outs],
        scratch_shapes=list(scratch),
        compiler_params=pltpu.CompilerParams(vmem_limit_bytes=VMEM_LIMIT),
        cost_estimate=pl.CostEstimate(
            flops=length * 10**9, bytes_accessed=0, transcendentals=0
        ),
    )(*scalars, *far, *arrays, *after)


def pinned(arrays):
    return [pltpu.with_memory_space_constraint(a, pltpu.HBM) for a in arrays]


def struct(shape, dtype):
    return jax.ShapeDtypeStruct(shape, dtype)


def swap(array, axis, bit):
    count = lax.axis_size(axis)
    return lax.ppermute(array, axis, [(i, i ^ bit) for i in range(count)])


def shifted(array, axis, by):
    count = lax.axis_size(axis)
    pairs = [(i, i + by) for i in range(count) if 0 <= i + by < count]
    return lax.ppermute(array, axis, pairs)


def spread(array):
    far = swap(array, "tp", 2)
    near = swap(array, "tp", 1)
    return array, near, far, swap(far, "tp", 1)


def mm(a, b):
    return jnp.dot(a, b, preferred_element_type=F32)


def mm_last(a, b):
    return lax.dot_general(a, b, (((1,), (1,)), ((), ())), preferred_element_type=F32)


def mm_first(a, b):
    return lax.dot_general(a, b, (((0,), (0,)), ((), ())), preferred_element_type=F32)


AHEAD = ((2, (0, 1, 2)), (3, (0, 1)), (3, (2,)))


def project_body(blocks, first, last, kinds, *refs):
    refs = list(refs)
    take = lambda count: [refs.pop(0) for _ in range(count)]
    mine = refs.pop(0)
    base = refs.pop(0) if last else None
    weights = take(3 if first else 1)
    (gain,) = take(1)
    pieces = take(len(blocks))
    accum, squares = take(2) if not first else (None, None)
    cosine, sine, asked = take(3) if last else (None, None, None)
    if first:
        held, sems = refs[-2:]
        del refs[-2:]
    rows, part = pieces[0].shape
    width = weights[0].shape[-1]
    copies = []
    onward = []
    if first:
        split_columns(mine, refs.pop(0), refs[-7:-3])
        for (block, needed), out in zip(AHEAD, refs[-3:]):
            at = pl.ds(pl.multiple_of((mine[0] ^ block) * part, part), part)
            onward += [
                pltpu.make_async_copy(weights[i].at[at, :], out.at[j], sems.at[i, block])
                for j, i in enumerate(needed)
            ]
        del refs[-7:]
    for i in range(3 if first else 0):
        for j, block in enumerate(blocks):
            at = pl.ds(pl.multiple_of((mine[0] ^ block) * part, part), part)
            copies.append(
                pltpu.make_async_copy(weights[i].at[at, :], held.at[i, j], sems.at[i, j])
            )
    for copy in copies + onward:
        copy.start()
    wide = [piece[...].astype(F32) for piece in pieces]
    total = sum(jnp.sum(w * w, axis=1, keepdims=True) for w in wide)
    if not first:
        total = total + squares[...]
    scaled = [
        (w * (gain[pl.ds(mine[0] ^ block, 1), :] * DAMP)).astype(BF16)
        for block, w in zip(blocks, wide)
    ]
    factor = lax.rsqrt(total / D + EPS) * (1.0 / DAMP)
    middle = HD // 2
    for i in kinds:
        place = kinds.index(i)
        at = slice(place * width, (place + 1) * width)
        field = 0.0
        for j, x in enumerate(scaled):
            if first:
                copies[i * len(blocks) + j].wait()
                field = field + mm(x, held[i, j])
            else:
                field = field + mm(x, weights[0][place])
        if not first:
            field = field + accum[:, at]
        if first:
            refs[-2][:, at] = field
            continue
        if not last:
            out = refs[-4] if i < 2 else refs[-2]
            out[:, at if i < 2 else slice(0, width)] = field
            continue
        field = (field * factor).T
        if 2 in kinds:
            query, own = refs[-2:]
        else:
            kv = refs[-4]
        for h in range(width // HD):
            at = h * HD
            a = field[at : at + middle]
            b = field[at + middle : at + HD]
            if i == 1:
                kv[2 * at + HD : 2 * at + 2 * HD, :] = field[at : at + HD].astype(BF16)
            else:
                to, out = (at, query) if i == 2 else (2 * at, kv)
                out[to : to + middle, :] = (a * cosine[...] - b * sine[...]).astype(BF16)
                out[to + middle : to + HD, :] = (b * cosine[...] + a * sine[...]).astype(BF16)
    if last and 2 not in kinds:
        refs[-3][...] = kv[...]
        refs[-2][...] = kv[...]
        refs[-1][...] = kv[:, rows // 2 :]
    if last and 2 in kinds:
        row = base[0] + lax.broadcasted_iota(jnp.int32, (rows, asked.shape[1]), 0)
        own[...] = mm(query[...], (asked[...] == row).astype(BF16)).astype(BF16)
    if not last:
        refs[-1][...] = total
        if not first:
            refs[-3][...] = total
    for copy in onward:
        copy.wait()


def project(
    blocks,
    mine,
    gain,
    pieces,
    weights,
    before=(),
    ending=None,
    after=(),
    length=0,
    kinds=(0, 1, 2),
    w_out=None,
):
    rows = pieces[0].shape[0]
    width = weights[0].shape[-1]
    scalars, arrays = [mine], [gain, *pieces, *before]
    if ending is None:
        outs = [struct((rows, 3 * width), F32), struct((rows, 1), F32)]
        if before:
            outs = [struct((rows, 2 * width), F32), struct((rows, 1), F32)]
            outs += [struct((rows, width), F32), struct((rows, 1), F32)]
    if not before:
        arrays.append(w_out)
        outs += [struct((w_out.shape[1] // 4, w_out.shape[0]), BF16)] * 4
        outs += [struct((len(n), pieces[0].shape[1], width), BF16) for _, n in AHEAD]
    if ending is not None:
        base, cosine, sine, asked = ending
        scalars.append(base)
        arrays += [cosine, sine, asked]
        outs = [struct((2 * width, rows), BF16)] * 3 + [struct((2 * width, rows // 2), BF16)]
        if 2 in kinds:
            outs = [struct((width, rows), BF16), struct((width, asked.shape[1]), BF16)]
    body = partial(project_body, blocks, not before, ending is not None, kinds)
    if before:
        arrays = list(weights) + arrays
        return call(body, outs, scalars, arrays, after, length=length)
    scratch = [
        pltpu.VMEM((3, len(blocks), pieces[0].shape[1], width), BF16),
        pltpu.SemaphoreType.DMA((3, 4)),
    ]
    return call(body, outs, scalars, arrays, after, scratch, length, weights)


def copy_body(source, *refs):
    refs[-1][...] = source[...]


def twice_body(source, *refs):
    refs[-2][...] = source[...]
    refs[-1][...] = source[...]


def prepare_body(base, lengths, segments, inverse, *refs):
    cosine, sine, low, asked_low = refs[-4:]
    prompts = lengths.shape[0]
    rows = segments.shape[1]
    segment = segments[...]
    asked = lax.broadcasted_iota(jnp.int32, asked_low.shape, 1)
    each = asked_low.shape[1] // prompts
    first = jnp.zeros((1, rows), jnp.int32)
    asked_first = jnp.zeros(asked_low.shape, jnp.int32)
    start = jnp.int32(0)
    for p in range(prompts):
        first = jnp.where(segment == p, start, first)
        asked_first = jnp.where(
            (asked >= p * each) & (asked < (p + 1) * each), start, asked_first
        )
        start = start + lengths[p]
    valid = segment >= 0
    slot = base[0] + lax.broadcasted_iota(jnp.int32, (1, rows), 1)
    position = jnp.where(valid, slot - first, 0).astype(F32)
    angles = inverse[...] * position
    cosine[...] = jnp.cos(angles)
    sine[...] = jnp.sin(angles)
    low[...] = jnp.where(valid, first - base[0], NEVER)
    asked_low[...] = asked_first - base[0]


def pick_body(base, slots, tokens, out):
    rows = tokens.shape[0]
    count = slots.shape[1]
    row = base[0] + lax.broadcasted_iota(jnp.int32, (rows, count), 0)
    out[...] = mm_first(tokens[...], (slots[...] == row).astype(BF16)).astype(BF16)


def add_body(first, second, *refs):
    refs[-1][...] = first[...] + second[...]


def request_body(count, low, high, block, *refs):
    query = sum(part[...] for part in refs[:count])
    width, rows = query.shape
    half = block.shape[1] // 2
    allowed = []
    for i in range(2):
        key_slot = i * half + lax.broadcasted_iota(jnp.int32, (half, rows), 0)
        allowed.append((key_slot >= low[...]) & (key_slot <= high[...]))
    results = []
    levels = []
    for h in range(width // HD):
        at = slice(h * HD, (h + 1) * HD)
        k_at = slice(2 * h * HD, (2 * h + 1) * HD)
        v_at = slice((2 * h + 1) * HD, (2 * h + 2) * HD)
        scores = [
            jnp.where(
                allowed[i], mm_first(block[k_at, i * half : (i + 1) * half], query[at, :]) * HD**-0.5, NEG
            )
            for i in range(2)
        ]
        largest = jnp.maximum(*[jnp.max(part, axis=0, keepdims=True) for part in scores])
        largest = jnp.maximum(largest, FLOOR)
        weights = [jnp.exp(part - largest) for part in scores]
        total = sum(jnp.sum(part, axis=0, keepdims=True) for part in weights)
        mixed = sum(
            mm(block[v_at, i * half : (i + 1) * half], weights[i].astype(BF16)) for i in range(2)
        )
        filled = total > 0
        safe = jnp.where(filled, total, 1.0)
        results.append((mixed * (1.0 / safe)).astype(BF16))
        levels.append(jnp.where(filled, largest + jnp.log(safe), NEG))
    out = refs[-1]
    for h, result in enumerate(results):
        out[h * HD : (h + 1) * HD, :] = result
    out[width:, :] = pack_levels(levels)


def pack_levels(levels):
    row = lax.broadcasted_iota(jnp.int32, (LEVEL_ROWS, levels[0].shape[1]), 0)
    packed = jnp.zeros(row.shape, F32)
    for h, level in enumerate(levels):
        for part in range(3):
            rounded = level.astype(BF16).astype(F32)
            packed = jnp.where(row == 3 * h + part, rounded, packed)
            level = level - rounded
    return packed.astype(BF16)


def combine_body(flip, own, other, *refs):
    width = own.shape[0] - LEVEL_ROWS
    turned = flip[0] > 0
    a = own[...].astype(F32)
    b = other[...].astype(F32)
    lower = jnp.where(turned, b, a)
    upper = jnp.where(turned, a, b)
    levels = []
    results = []
    for h in range(width // HD):
        marks = []
        for side in (lower, upper):
            at = width + 3 * h
            marks.append(side[at : at + 1] + side[at + 1 : at + 2] + side[at + 2 : at + 3])
        top = jnp.maximum(*marks)
        one, two = (jnp.exp(mark - top) for mark in marks)
        both = one + two
        levels.append(top + jnp.log(both))
        at = slice(h * HD, (h + 1) * HD)
        results.append((lower[at] * (one / both) + upper[at] * (two / both)).astype(BF16))
    out = refs[-1]
    for h, result in enumerate(results):
        out[h * HD : (h + 1) * HD, :] = result
    if out.shape[0] > width:
        out[width:, :] = pack_levels(levels)


def combine(flip, own, other, rows, after=()):
    return call(
        combine_body,
        [struct((rows, own.shape[1]), BF16)],
        [flip],
        [own, other],
        after,
        length=3,
        blocked=True,
    )[0]


def attend_body(sources, last, place, low, query, *refs):
    width, rows = query.shape
    half = rows // 2
    heads = width // HD
    blocks = refs[: len(sources)]
    state = refs[len(sources) :]
    accum, largest, total = refs[-3:]
    if sources[0][0] == 0:
        accum[...] = jnp.zeros(accum.shape, F32)
        largest[...] = jnp.full(largest.shape, FLOOR, F32)
        total[...] = jnp.zeros(total.shape, F32)
    else:
        accum[...] = state[0][...]
        largest[...] = state[1][...]
        total[...] = state[2][...]

    def visit(distance, block, part, i, until, j):
        q_at = slice(i * half, until * half)
        k_half = slice(part * half, (part + 1) * half)
        shape = (half, (until - i) * half)
        key_slot = (
            j * half - distance * rows + lax.broadcasted_iota(jnp.int32, shape, 0)
        )
        allowed = key_slot >= low[:, q_at]
        if distance == 0:
            query_slot = i * half + lax.broadcasted_iota(jnp.int32, shape, 1)
            allowed = allowed & (key_slot <= query_slot)
        scores = [
            mm_first(
                block[2 * h * HD : (2 * h + 1) * HD, k_half],
                query[h * HD : (h + 1) * HD, q_at],
            )
            for h in range(heads)
        ]
        parts = []
        for h in range(heads):
            score = jnp.where(allowed, scores[h] * (HD**-0.5 * LOG2_E), NEG)
            m_old = largest[h : h + 1, q_at]
            m_new = jnp.maximum(m_old, jnp.max(score, axis=0, keepdims=True))
            parts.append((m_new, jnp.exp2(score - m_new), jnp.exp2(m_old - m_new)))
        done = []
        for h, (m_new, weights, factor) in enumerate(parts):
            v_at = slice((2 * h + 1) * HD, (2 * h + 2) * HD)
            t_new = total[h : h + 1, q_at] * factor + jnp.sum(weights, axis=0, keepdims=True)
            mixed = accum[h * HD : (h + 1) * HD, q_at] * factor + mm(
                block[v_at, k_half], weights.astype(BF16)
            )
            done.append((m_new, t_new, mixed))
        for h, (m_new, t_new, mixed) in enumerate(done):
            accum[h * HD : (h + 1) * HD, q_at] = mixed
            largest[h : h + 1, q_at] = m_new
            total[h : h + 1, q_at] = t_new

    limits = [jnp.min(low[:, i * half : (i + 1) * half]) for i in range(2)]
    for (distance, least, most, skipped), block in zip(sources, blocks):
        here = (place[0] >= least) & (place[0] <= most)
        for j in range(skipped, 2):
            end = (j + 1) * half - distance * rows
            look = partial(visit, distance, block, j - skipped)
            if distance == 0 and j == 1:
                pl.when(limits[1] < end)(partial(look, 1, 2, j))
            else:
                pl.when(here & (limits[1] < end))(partial(look, 0, 2, j))
                pl.when(here & (limits[1] >= end) & (limits[0] < end))(partial(look, 0, 1, j))
    if last:
        out = refs[-4]
        for h in range(heads):
            at = slice(h * HD, (h + 1) * HD)
            t_h = total[h : h + 1, :]
            accum[at, :] = accum[at, :] * (1.0 / jnp.where(t_h > 0, t_h, 1.0))
        out[...] = accum[...].T.astype(BF16)


def attend(sources, last, place, low, query, blocks, state, length=0, after=()):
    width, rows = query.shape
    shapes = [struct((width, rows), F32), struct((8, rows), F32), struct((8, rows), F32)]
    scratch = []
    outs = shapes
    if last:
        scratch = [pltpu.VMEM(s.shape, s.dtype) for s in shapes]
        outs = [struct((rows, width), BF16)]
    return call(
        partial(attend_body, sources, last),
        outs,
        [place],
        [low, query, *blocks, *state],
        after,
        scratch,
        length,
        blocked=True,
    )


def begin_body(limit, start, vocab, weight_far, tail, tokens, own, near, near_weight, *refs):
    half, base, weight, sems = refs[-4:]
    rows = half.shape[0]
    whole_rows = (limit - rows) // 16 * 16
    lower = start[0] == 0

    def fetch(at, count):
        return pltpu.make_async_copy(
            vocab.at[pl.ds(at, count), :], half.at[pl.ds(0, count), :], sems.at[0]
        )

    load = pltpu.make_async_copy(weight_far, weight, sems.at[1])
    load.start()

    @pl.when(lower)
    def _():
        fetch(0, rows).start()

    @pl.when(jnp.logical_not(lower))
    def _():
        fetch(rows, whole_rows).start()

    field = tokens[...].astype(F32) + mm(near_weight[...], near[...]).astype(BF16).astype(F32)
    load.wait()
    base[...] = field + mm(weight[...], own[...]).astype(BF16).astype(F32)

    @pl.when(lower)
    def _():
        fetch(0, rows).wait()

    @pl.when(jnp.logical_not(lower))
    def _():
        fetch(rows, whole_rows).wait()
        if limit > rows + whole_rows:
            half[whole_rows : whole_rows + 16, :] = tail[...]


def begin_rows(start, vocab, weight_far, tokens, own, near, near_weight):
    limit, width = vocab.shape
    count = tokens.shape[1]
    rows = pl.cdiv(limit, 4 * 32) * 64
    last_tile = (limit - 1) // 16
    return pl.pallas_call(
        partial(begin_body, limit),
        grid=(1,),
        out_shape=[struct((rows, width), BF16), struct((width, count), F32)],
        in_specs=[SCALARS, FAR_MEMORY, FAR_MEMORY]
        + [pl.BlockSpec((16, width), lambda i: (last_tile, 0))]
        + [whole(a) for a in (tokens, own, near, near_weight)],
        out_specs=[WHOLE, whole(tokens)],
        scratch_shapes=[pltpu.VMEM(weight_far.shape, BF16), pltpu.SemaphoreType.DMA((2,))],
        compiler_params=pltpu.CompilerParams(vmem_limit_bytes=VMEM_LIMIT),
        cost_estimate=pl.CostEstimate(flops=0, bytes_accessed=0, transcendentals=0),
    )(start, vocab, weight_far, vocab, tokens, own, near, near_weight)


def rows_body(gain_far, base, far, last, far_weight, last_weight, *refs):
    squares, scaled, again, gain, sem = refs[-5:]
    copy = pltpu.make_async_copy(gain_far, gain, sem.at[0])
    copy.start()
    rows = base[...] + mm(far_weight[...], far[...]).astype(BF16).astype(F32)
    rows = rows + mm(last_weight[...], last[...]).astype(BF16).astype(F32)
    squares[...] = jnp.sum(rows * rows, axis=0, keepdims=True)
    copy.wait()
    scaled[...] = (rows * (gain[...] * SHRINK)).astype(BF16)
    again[...] = scaled[...]


def held_body(limit, start, half, scaled, out):
    row = start[0] + lax.broadcasted_iota(jnp.int32, out.shape, 0)
    out[...] = jnp.where(row < limit, mm(half[...], scaled[...]), NEG).astype(BF16)


def logits_body(limit, start, vocab, scaled, *refs):
    out = refs[-1]
    first = (start[0] + pl.program_id(0)) * out.shape[0]
    row = first + lax.broadcasted_iota(jnp.int32, out.shape, 0)
    out[...] = jnp.where(row < limit, mm(vocab[...], scaled[...]), NEG).astype(BF16)


def half_logits(start, vocab, scaled, after=()):
    limit, width = vocab.shape
    count = scaled.shape[1]
    tile = pl.cdiv(limit, 4 * 32) * 32
    return pl.pallas_call(
        partial(logits_body, limit),
        grid_spec=pltpu.PrefetchScalarGridSpec(
            num_scalar_prefetch=1,
            grid=(2,),
            in_specs=[
                pl.BlockSpec((tile, width), lambda i, start: (start[0] + i, 0)),
                pl.BlockSpec((width, count), lambda i, start: (0, 0)),
            ]
            + [ANYWHERE] * len(after),
            out_specs=pl.BlockSpec((tile, count), lambda i, start: (i, 0)),
        ),
        out_shape=struct((2 * tile, count), BF16),
        compiler_params=pltpu.CompilerParams(vmem_limit_bytes=VMEM_LIMIT),
        cost_estimate=pl.CostEstimate(flops=0, bytes_accessed=0, transcendentals=0),
    )(start, vocab, scaled, *after)


def fold_body(side, kept, came, send, keep):
    quarter = send.shape[0]
    for out, turn in ((send, 1 - side[0]), (keep, side[0])):
        at = pl.ds(pl.multiple_of(turn * quarter, 16), quarter)
        out[...] = (kept[at, :].astype(F32) + came[at, :].astype(F32)).astype(out.dtype)


def top_body(kept, came, *refs):
    out = refs[-1]
    out[...] = jnp.max(kept[...] + came[...].astype(F32), axis=0, keepdims=True)


def pair_body(first, second, *refs):
    refs[-1][0:1, :] = first[...]
    refs[-1][1:2, :] = second[...]


def split_columns(mine, source, outs):
    width = outs[0].shape[0]
    for b in range(4):
        at = pl.ds(pl.multiple_of((mine[0] ^ b) * width, width), width)
        outs[b][...] = source[:, at].T


def shards(
    tokens,
    norm_gain,
    w_query,
    w_key,
    w_value,
    w_out,
    final_gain,
    w_vocab,
    segment_ids,
    prompt_lengths,
    request_slots,
):
    rows, columns = tokens.shape
    half = rows // 2
    width = w_query.shape[1]
    heads = width // HD
    n_seq = lax.axis_size("seq")
    span = n_seq // 4
    seq_index = lax.axis_index("seq")
    tp_index = lax.axis_index("tp")
    mine = tp_index.reshape(1)
    base = seq_index * rows
    requests = request_slots.shape[0]
    prompts = prompt_lengths.shape[0]

    far = swap(tokens, "tp", 2)
    pieces = [tokens, swap(tokens, "tp", 1), far]
    gain = norm_gain.reshape(4, columns)
    weights = [
        pltpu.with_memory_space_constraint(w, pltpu.HBM) for w in (w_key, w_value, w_query)
    ]
    *sums, w_split, w_1, w_2, w_3, far_weights, last_kv, last_query = project(
        (0, 1), mine, gain, pieces[:2], weights, w_out=w_out
    )
    w_parts = [w_split] + [swap(w, "tp", b) for b, w in ((1, w_1), (2, w_2), (3, w_3))]
    powers = np.arange(HD // 2, dtype=np.float32) * np.float32(2.0 / HD)
    inverse = (np.float32(10000.0) ** -powers).astype(np.float32)[:, None]
    cosine, sine, low, request_low = call(
        prepare_body,
        [
            struct((HD // 2, rows), F32),
            struct((HD // 2, rows), F32),
            struct((1, rows), jnp.int32),
            struct((1, requests), jnp.int32),
        ],
        [base.reshape(1), prompt_lengths],
        pinned([segment_ids[None, :], jnp.asarray(inverse)]),
        sums[1:2],
        blocked=True,
    )
    last_gain = final_gain[:, None]
    relayed, far = call(
        twice_body, [struct(far.shape, BF16)] * 2, [], [far], (sums[1], cosine, last_gain)
    )
    pieces = pieces[:2] + [far, swap(relayed, "tp", 1)]

    asked = request_slots[None, :]
    inside = asked - base
    (own_tokens,) = call(
        pick_body, [struct((columns, requests), BF16)], [base.reshape(1)], pinned([asked, tokens]),
        blocked=True,
    )
    all_tokens = [own_tokens]
    *kv_sums, query_sums, query_squares = project(
        (2,), mine, gain, pieces[2:3], [far_weights], sums, None, (), length=10
    )
    ending = (base.reshape(1), cosine, sine, asked)
    query, own_query = project(
        (3,), mine, gain, pieces[3:], [last_query], (query_sums, query_squares), ending, (), 2, (2,)
    )
    asking = [own_query] + [shifted(own_query, "seq", -by) for by in range(1, span + 1)]
    bit = n_seq // 2
    while bit:
        all_tokens += call(
            add_body,
            [struct(own_tokens.shape, BF16)],
            [],
            [all_tokens[-1], swap(all_tokens[-1], "seq", bit)],
            sums[1:2] if len(all_tokens) == 1 else (own_query,),
        )
        bit //= 2
    asked_kv, own_kv, kv, kv_half = project(
        (3,),
        mine,
        gain,
        pieces[3:],
        [last_kv],
        kv_sums,
        ending,
        (own_query,),
        10,
        (0, 1),
    )

    kv_cache = jnp.transpose(kv.reshape(heads, 2 * HD, rows), (0, 2, 1))
    behind = shifted(kv, "seq", 1)

    last_start = n_seq - span - 1
    ends = jnp.cumsum(prompt_lengths)
    reach = (ends - 1) // rows - (ends - prompt_lengths) // rows
    longest = jnp.max(jnp.where(jnp.arange(prompts) < prompts - 1, reach, 0))
    sources = [(0, 0, n_seq, 0), (1, 0, n_seq, 0)]
    blocks = [own_kv, behind]
    for by in range(2, span + 1):
        early = [(i, i + by) for i in range(last_start + 1 - by)]
        late = [(i, i + by) for i in range(last_start, n_seq - by)]
        sources.append((by, 0, last_start, 0))
        blocks.append(
            lax.cond(
                longest >= by,
                lambda array, pairs=early: lax.ppermute(array, "seq", pairs),
                jnp.zeros_like,
                kv,
            )
        )
        from_half = 1 if by == span else 0
        sources.append((by, last_start + by, n_seq, from_half))
        blocks.append(lax.ppermute(kv_half if from_half else kv, "seq", late))
    halo = tuple(blocks[2:4])

    (mixed,) = call(
        partial(request_body, len(asking)),
        [struct((width + LEVEL_ROWS, requests), BF16)],
        [],
        [request_low, inside, asked_kv, *asking],
        all_tokens[2:3],
    )
    afters = [
        all_tokens[3:4] + w_parts[2:3] + [halo[1]],
        halo[:1],
        w_parts[3:4] + [all_tokens[-1]],
    ]
    bit = 1
    while bit < n_seq:
        flip = ((seq_index & bit) > 0).astype(jnp.int32).reshape(1)
        after = afters.pop(0) if afters else ()
        other = swap(mixed, "seq", bit)
        bit *= 2
        kept_rows = width + LEVEL_ROWS if bit < n_seq else width
        mixed = combine(flip, mixed, other, kept_rows, after)
    _, near_mixed, far_mixed, last_mixed = spread(mixed)

    core = tp_index & 1
    side = tp_index >> 1
    vocab = pltpu.with_memory_space_constraint(w_vocab.T, pltpu.HBM)
    limit = vocab.shape[0]
    vocab_rows = pl.cdiv(limit, 4 * 32) * 64
    away = (vocab_rows * (1 - core)).reshape(1)
    far_gain, own_weight = pinned([last_gain, w_split])
    held, field = begin_rows(
        away, vocab, own_weight, all_tokens[-1], mixed, near_mixed, w_parts[1]
    )
    squares, scaled, again = call(
        rows_body,
        [struct((1, requests), F32)] + [struct(own_tokens.shape, BF16)] * 2,
        [],
        [field, far_mixed, last_mixed, *w_parts[2:]],
        scratch=[pltpu.VMEM((columns, 1), F32), pltpu.SemaphoreType.DMA((1,))],
        far=[far_gain],
    )
    (sent,) = call(
        partial(held_body, limit),
        [struct((vocab_rows, requests), BF16)],
        [away],
        [held, scaled],
    )
    kept = half_logits((2 * core).reshape(1), vocab, again, (sent,))
    quarter = kept.shape[0] // 2
    sent, kept = call(
        fold_body,
        [struct((quarter, requests), BF16), struct((quarter, requests), F32)],
        [side.reshape(1)],
        [kept, swap(sent, "tp", 1)],
    )
    state = ()
    while sources:
        last = len(sources) <= 4
        state = attend(
            sources[:4], last, seq_index.reshape(1), low, query, blocks[:4], state, 30
        )
        sources, blocks = sources[4:], blocks[4:]
    (best,) = call(
        top_body, [struct((1, requests), F32)], [], [kept, swap(sent, "tp", 2)], state[:1]
    )
    bit = 1
    while bit < n_seq:
        best = jnp.maximum(best, swap(best, "seq", bit))
        bit *= 2
    attended = spread(state[0])
    (pair,) = call(
        pair_body, [struct((2, requests), F32)], [], [best, squares], attended[2:3]
    )
    for bit in (2, 1):
        other = swap(pair, "tp", bit)
        pair = jnp.stack([jnp.maximum(pair[0], other[0]), pair[1] + other[1]])
    hidden_norm = jnp.sqrt(pair[1] / D + EPS)
    top_logit = pair[0] / hidden_norm * (1.0 / SHRINK)

    summed = sum(
        mm_last(part, w).astype(BF16).astype(F32) for part, w in zip(attended, w_parts)
    )
    hidden = (tokens.astype(F32) + summed).astype(BF16)
    return (kv_cache, hidden, hidden_norm, top_logit)


def solution(mesh):
    return jax.shard_map(
        shards,
        mesh=mesh,
        in_specs=(
            P("seq", "tp"),
            P(),
            P(None, "tp"),
            P(None, "tp"),
            P(None, "tp"),
            P("tp", None),
            P("tp"),
            P("tp", "seq"),
            P("seq"),
            P(),
            P(),
        ),
        out_specs=(P("tp", "seq", None), P("seq", "tp"), P(), P()),
        check_vma=False,
    )
```

```python
from functools import partial

import jax
import jax.numpy as jnp
import numpy as np
from jax import lax
from jax.experimental import pallas as pl
from jax.experimental.pallas import tpu as pltpu
from jax.sharding import PartitionSpec as P

D = 3072
HD = 96
EPS = 1e-05
NEG = -1e30
FLOOR = -5e29
NEVER = 2**30
LEVEL_ROWS = 16
SHRINK = 2.0**-16
DAMP = 2.0**-24
LOG2_E = 1.4426950408889634
F32 = jnp.float32
BF16 = jnp.bfloat16
VMEM_LIMIT = 12 * 1024 * 1024

SCALARS = pl.BlockSpec(memory_space=pltpu.SMEM)
ANYWHERE = pl.BlockSpec(memory_space=pl.ANY)
FAR_MEMORY = pl.BlockSpec(memory_space=pltpu.HBM)


WHOLE = pl.BlockSpec(memory_space=pltpu.VMEM)


def whole(array):
    return pl.BlockSpec(array.shape, lambda i: (0, 0), pipeline_mode=pl.Buffered(1))


def call(body, outs, scalars, arrays, after=(), scratch=(), length=0, far=(), blocked=False):
    return pl.pallas_call(
        body,
        grid=(1,) if blocked else (),
        out_shape=outs,
        in_specs=[SCALARS] * len(scalars)
        + [FAR_MEMORY] * len(far)
        + [whole(array) if blocked else WHOLE for array in arrays]
        + [ANYWHERE] * len(after),
        out_specs=[whole(out) if blocked else WHOLE for out in outs],
        scratch_shapes=list(scratch),
        compiler_params=pltpu.CompilerParams(vmem_limit_bytes=VMEM_LIMIT),
        cost_estimate=pl.CostEstimate(
            flops=length * 10**9, bytes_accessed=0, transcendentals=0
        ),
    )(*scalars, *far, *arrays, *after)


def pinned(arrays):
    return [pltpu.with_memory_space_constraint(a, pltpu.HBM) for a in arrays]


def struct(shape, dtype):
    return jax.ShapeDtypeStruct(shape, dtype)


def swap(array, axis, bit):
    count = lax.axis_size(axis)
    return lax.ppermute(array, axis, [(i, i ^ bit) for i in range(count)])


def shifted(array, axis, by):
    count = lax.axis_size(axis)
    pairs = [(i, i + by) for i in range(count) if 0 <= i + by < count]
    return lax.ppermute(array, axis, pairs)


def spread(array):
    far = swap(array, "tp", 2)
    near = swap(array, "tp", 1)
    return array, near, far, swap(far, "tp", 1)


def mm(a, b):
    return jnp.dot(a, b, preferred_element_type=F32)


def mm_last(a, b):
    return lax.dot_general(a, b, (((1,), (1,)), ((), ())), preferred_element_type=F32)


def mm_first(a, b):
    return lax.dot_general(a, b, (((0,), (0,)), ((), ())), preferred_element_type=F32)


AHEAD = ((2, (0, 1, 2)), (3, (0, 1)), (3, (2,)))


def project_body(blocks, first, last, kinds, *refs):
    refs = list(refs)
    take = lambda count: [refs.pop(0) for _ in range(count)]
    mine = refs.pop(0)
    base = refs.pop(0) if last else None
    weights = take(3 if first else 1)
    (gain,) = take(1)
    pieces = take(len(blocks))
    accum, squares = take(2) if not first else (None, None)
    cosine, sine, asked = take(3) if last else (None, None, None)
    if first:
        held, sems = refs[-2:]
        del refs[-2:]
    rows, part = pieces[0].shape
    width = weights[0].shape[-1]
    copies = []
    onward = []
    if first:
        split_columns(mine, refs.pop(0), refs[-7:-3])
        for (block, needed), out in zip(AHEAD, refs[-3:]):
            at = pl.ds(pl.multiple_of((mine[0] ^ block) * part, part), part)
            onward += [
                pltpu.make_async_copy(weights[i].at[at, :], out.at[j], sems.at[i, block])
                for j, i in enumerate(needed)
            ]
        del refs[-7:]
    for i in range(3 if first else 0):
        for j, block in enumerate(blocks):
            at = pl.ds(pl.multiple_of((mine[0] ^ block) * part, part), part)
            copies.append(
                pltpu.make_async_copy(weights[i].at[at, :], held.at[i, j], sems.at[i, j])
            )
    for copy in copies + onward:
        copy.start()
    wide = [piece[...].astype(F32) for piece in pieces]
    total = sum(jnp.sum(w * w, axis=1, keepdims=True) for w in wide)
    if not first:
        total = total + squares[...]
    scaled = [
        (w * (gain[pl.ds(mine[0] ^ block, 1), :] * DAMP)).astype(BF16)
        for block, w in zip(blocks, wide)
    ]
    factor = lax.rsqrt(total / D + EPS) * (1.0 / DAMP)
    middle = HD // 2
    for i in kinds:
        place = kinds.index(i)
        at = slice(place * width, (place + 1) * width)
        field = 0.0
        for j, x in enumerate(scaled):
            if first:
                copies[i * len(blocks) + j].wait()
                field = field + mm(x, held[i, j])
            else:
                field = field + mm(x, weights[0][place])
        if not first:
            field = field + accum[:, at]
        if first:
            refs[-2][:, at] = field
            continue
        if not last:
            out = refs[-4] if i < 2 else refs[-2]
            out[:, at if i < 2 else slice(0, width)] = field
            continue
        field = (field * factor).T
        if 2 in kinds:
            query, own = refs[-2:]
        else:
            kv = refs[-4]
        for h in range(width // HD):
            at = h * HD
            a = field[at : at + middle]
            b = field[at + middle : at + HD]
            if i == 1:
                kv[2 * at + HD : 2 * at + 2 * HD, :] = field[at : at + HD].astype(BF16)
            else:
                to, out = (at, query) if i == 2 else (2 * at, kv)
                out[to : to + middle, :] = (a * cosine[...] - b * sine[...]).astype(BF16)
                out[to + middle : to + HD, :] = (b * cosine[...] + a * sine[...]).astype(BF16)
    if last and 2 not in kinds:
        refs[-3][...] = kv[...]
        refs[-2][...] = kv[...]
        refs[-1][...] = kv[:, rows // 2 :]
    if last and 2 in kinds:
        row = base[0] + lax.broadcasted_iota(jnp.int32, (rows, asked.shape[1]), 0)
        own[...] = mm(query[...], (asked[...] == row).astype(BF16)).astype(BF16)
    if not last:
        refs[-1][...] = total
        if not first:
            refs[-3][...] = total
    for copy in onward:
        copy.wait()


def project(
    blocks,
    mine,
    gain,
    pieces,
    weights,
    before=(),
    ending=None,
    after=(),
    length=0,
    kinds=(0, 1, 2),
    w_out=None,
):
    rows = pieces[0].shape[0]
    width = weights[0].shape[-1]
    scalars, arrays = [mine], [gain, *pieces, *before]
    if ending is None:
        outs = [struct((rows, 3 * width), F32), struct((rows, 1), F32)]
        if before:
            outs = [struct((rows, 2 * width), F32), struct((rows, 1), F32)]
            outs += [struct((rows, width), F32), struct((rows, 1), F32)]
    if not before:
        arrays.append(w_out)
        outs += [struct((w_out.shape[1] // 4, w_out.shape[0]), BF16)] * 4
        outs += [struct((len(n), pieces[0].shape[1], width), BF16) for _, n in AHEAD]
    if ending is not None:
        base, cosine, sine, asked = ending
        scalars.append(base)
        arrays += [cosine, sine, asked]
        outs = [struct((2 * width, rows), BF16)] * 3 + [struct((2 * width, rows // 2), BF16)]
        if 2 in kinds:
            outs = [struct((width, rows), BF16), struct((width, asked.shape[1]), BF16)]
    body = partial(project_body, blocks, not before, ending is not None, kinds)
    if before:
        arrays = list(weights) + arrays
        return call(body, outs, scalars, arrays, after, length=length)
    scratch = [
        pltpu.VMEM((3, len(blocks), pieces[0].shape[1], width), BF16),
        pltpu.SemaphoreType.DMA((3, 4)),
    ]
    return call(body, outs, scalars, arrays, after, scratch, length, weights)


def copy_body(source, *refs):
    refs[-1][...] = source[...]


def twice_body(source, *refs):
    refs[-2][...] = source[...]
    refs[-1][...] = source[...]


def prepare_body(base, lengths, segments, inverse, *refs):
    cosine, sine, low, asked_low = refs[-4:]
    prompts = lengths.shape[0]
    rows = segments.shape[1]
    segment = segments[...]
    asked = lax.broadcasted_iota(jnp.int32, asked_low.shape, 1)
    each = asked_low.shape[1] // prompts
    first = jnp.zeros((1, rows), jnp.int32)
    asked_first = jnp.zeros(asked_low.shape, jnp.int32)
    start = jnp.int32(0)
    for p in range(prompts):
        first = jnp.where(segment == p, start, first)
        asked_first = jnp.where(
            (asked >= p * each) & (asked < (p + 1) * each), start, asked_first
        )
        start = start + lengths[p]
    valid = segment >= 0
    slot = base[0] + lax.broadcasted_iota(jnp.int32, (1, rows), 1)
    position = jnp.where(valid, slot - first, 0).astype(F32)
    angles = inverse[...] * position
    cosine[...] = jnp.cos(angles)
    sine[...] = jnp.sin(angles)
    low[...] = jnp.where(valid, first - base[0], NEVER)
    asked_low[...] = asked_first - base[0]


def pick_body(base, slots, tokens, out):
    rows = tokens.shape[0]
    count = slots.shape[1]
    row = base[0] + lax.broadcasted_iota(jnp.int32, (rows, count), 0)
    out[...] = mm_first(tokens[...], (slots[...] == row).astype(BF16)).astype(BF16)


def add_body(first, second, *refs):
    refs[-1][...] = first[...] + second[...]


def request_body(count, low, high, block, *refs):
    query = sum(part[...] for part in refs[:count])
    width, rows = query.shape
    half = block.shape[1] // 2
    allowed = []
    for i in range(2):
        key_slot = i * half + lax.broadcasted_iota(jnp.int32, (half, rows), 0)
        allowed.append((key_slot >= low[...]) & (key_slot <= high[...]))
    results = []
    levels = []
    for h in range(width // HD):
        at = slice(h * HD, (h + 1) * HD)
        k_at = slice(2 * h * HD, (2 * h + 1) * HD)
        v_at = slice((2 * h + 1) * HD, (2 * h + 2) * HD)
        scores = [
            jnp.where(
                allowed[i], mm_first(block[k_at, i * half : (i + 1) * half], query[at, :]) * HD**-0.5, NEG
            )
            for i in range(2)
        ]
        largest = jnp.maximum(*[jnp.max(part, axis=0, keepdims=True) for part in scores])
        largest = jnp.maximum(largest, FLOOR)
        weights = [jnp.exp(part - largest) for part in scores]
        total = sum(jnp.sum(part, axis=0, keepdims=True) for part in weights)
        mixed = sum(
            mm(block[v_at, i * half : (i + 1) * half], weights[i].astype(BF16)) for i in range(2)
        )
        filled = total > 0
        safe = jnp.where(filled, total, 1.0)
        results.append((mixed * (1.0 / safe)).astype(BF16))
        levels.append(jnp.where(filled, largest + jnp.log(safe), NEG))
    out = refs[-1]
    for h, result in enumerate(results):
        out[h * HD : (h + 1) * HD, :] = result
    out[width:, :] = pack_levels(levels)


def pack_levels(levels):
    row = lax.broadcasted_iota(jnp.int32, (LEVEL_ROWS, levels[0].shape[1]), 0)
    packed = jnp.zeros(row.shape, F32)
    for h, level in enumerate(levels):
        for part in range(3):
            rounded = level.astype(BF16).astype(F32)
            packed = jnp.where(row == 3 * h + part, rounded, packed)
            level = level - rounded
    return packed.astype(BF16)


def combine_body(flip, own, other, *refs):
    width = own.shape[0] - LEVEL_ROWS
    turned = flip[0] > 0
    a = own[...].astype(F32)
    b = other[...].astype(F32)
    lower = jnp.where(turned, b, a)
    upper = jnp.where(turned, a, b)
    levels = []
    results = []
    for h in range(width // HD):
        marks = []
        for side in (lower, upper):
            at = width + 3 * h
            marks.append(side[at : at + 1] + side[at + 1 : at + 2] + side[at + 2 : at + 3])
        top = jnp.maximum(*marks)
        one, two = (jnp.exp(mark - top) for mark in marks)
        both = one + two
        levels.append(top + jnp.log(both))
        at = slice(h * HD, (h + 1) * HD)
        results.append((lower[at] * (one / both) + upper[at] * (two / both)).astype(BF16))
    out = refs[-1]
    for h, result in enumerate(results):
        out[h * HD : (h + 1) * HD, :] = result
    if out.shape[0] > width:
        out[width:, :] = pack_levels(levels)


def combine(flip, own, other, rows, after=()):
    return call(
        combine_body,
        [struct((rows, own.shape[1]), BF16)],
        [flip],
        [own, other],
        after,
        length=3,
        blocked=True,
    )[0]


def attend_body(sources, last, place, low, query, *refs):
    width, rows = query.shape
    half = rows // 2
    heads = width // HD
    blocks = refs[: len(sources)]
    state = refs[len(sources) :]
    accum, largest, total = refs[-3:]
    if sources[0][0] == 0:
        accum[...] = jnp.zeros(accum.shape, F32)
        largest[...] = jnp.full(largest.shape, FLOOR, F32)
        total[...] = jnp.zeros(total.shape, F32)
    else:
        accum[...] = state[0][...]
        largest[...] = state[1][...]
        total[...] = state[2][...]

    def visit(distance, block, part, i, until, j):
        q_at = slice(i * half, until * half)
        k_half = slice(part * half, (part + 1) * half)
        shape = (half, (until - i) * half)
        key_slot = (
            j * half - distance * rows + lax.broadcasted_iota(jnp.int32, shape, 0)
        )
        allowed = key_slot >= low[:, q_at]
        if distance == 0:
            query_slot = i * half + lax.broadcasted_iota(jnp.int32, shape, 1)
            allowed = allowed & (key_slot <= query_slot)
        scores = [
            mm_first(
                block[2 * h * HD : (2 * h + 1) * HD, k_half],
                query[h * HD : (h + 1) * HD, q_at],
            )
            for h in range(heads)
        ]
        parts = []
        for h in range(heads):
            score = jnp.where(allowed, scores[h] * (HD**-0.5 * LOG2_E), NEG)
            m_old = largest[h : h + 1, q_at]
            m_new = jnp.maximum(m_old, jnp.max(score, axis=0, keepdims=True))
            parts.append((m_new, jnp.exp2(score - m_new), jnp.exp2(m_old - m_new)))
        done = []
        for h, (m_new, weights, factor) in enumerate(parts):
            v_at = slice((2 * h + 1) * HD, (2 * h + 2) * HD)
            t_new = total[h : h + 1, q_at] * factor + jnp.sum(weights, axis=0, keepdims=True)
            mixed = accum[h * HD : (h + 1) * HD, q_at] * factor + mm(
                block[v_at, k_half], weights.astype(BF16)
            )
            done.append((m_new, t_new, mixed))
        for h, (m_new, t_new, mixed) in enumerate(done):
            accum[h * HD : (h + 1) * HD, q_at] = mixed
            largest[h : h + 1, q_at] = m_new
            total[h : h + 1, q_at] = t_new

    limits = [jnp.min(low[:, i * half : (i + 1) * half]) for i in range(2)]
    for (distance, least, most, skipped), block in zip(sources, blocks):
        here = (place[0] >= least) & (place[0] <= most)
        for j in range(skipped, 2):
            end = (j + 1) * half - distance * rows
            look = partial(visit, distance, block, j - skipped)
            if distance == 0 and j == 1:
                pl.when(limits[1] < end)(partial(look, 1, 2, j))
            else:
                pl.when(here & (limits[1] < end))(partial(look, 0, 2, j))
                pl.when(here & (limits[1] >= end) & (limits[0] < end))(partial(look, 0, 1, j))
    if last:
        out = refs[-4]
        for h in range(heads):
            at = slice(h * HD, (h + 1) * HD)
            t_h = total[h : h + 1, :]
            accum[at, :] = accum[at, :] * (1.0 / jnp.where(t_h > 0, t_h, 1.0))
        out[...] = accum[...].T.astype(BF16)


def attend(sources, last, place, low, query, blocks, state, length=0, after=()):
    width, rows = query.shape
    shapes = [struct((width, rows), F32), struct((8, rows), F32), struct((8, rows), F32)]
    scratch = []
    outs = shapes
    if last:
        scratch = [pltpu.VMEM(s.shape, s.dtype) for s in shapes]
        outs = [struct((rows, width), BF16)]
    return call(
        partial(attend_body, sources, last),
        outs,
        [place],
        [low, query, *blocks, *state],
        after,
        scratch,
        length,
        blocked=True,
    )


def begin_body(limit, start, vocab, weight_far, tail, tokens, own, near, near_weight, *refs):
    half, base, weight, sems = refs[-4:]
    rows = half.shape[0]
    whole_rows = (limit - rows) // 16 * 16
    lower = start[0] == 0

    def fetch(at, count):
        return pltpu.make_async_copy(
            vocab.at[pl.ds(at, count), :], half.at[pl.ds(0, count), :], sems.at[0]
        )

    load = pltpu.make_async_copy(weight_far, weight, sems.at[1])
    load.start()

    @pl.when(lower)
    def _():
        fetch(0, rows).start()

    @pl.when(jnp.logical_not(lower))
    def _():
        fetch(rows, whole_rows).start()

    field = tokens[...].astype(F32) + mm(near_weight[...], near[...]).astype(BF16).astype(F32)
    load.wait()
    base[...] = field + mm(weight[...], own[...]).astype(BF16).astype(F32)

    @pl.when(lower)
    def _():
        fetch(0, rows).wait()

    @pl.when(jnp.logical_not(lower))
    def _():
        fetch(rows, whole_rows).wait()
        if limit > rows + whole_rows:
            half[whole_rows : whole_rows + 16, :] = tail[...]


def begin_rows(start, vocab, weight_far, tokens, own, near, near_weight):
    limit, width = vocab.shape
    count = tokens.shape[1]
    rows = pl.cdiv(limit, 4 * 32) * 64
    last_tile = (limit - 1) // 16
    return pl.pallas_call(
        partial(begin_body, limit),
        grid=(1,),
        out_shape=[struct((rows, width), BF16), struct((width, count), F32)],
        in_specs=[SCALARS, FAR_MEMORY, FAR_MEMORY]
        + [pl.BlockSpec((16, width), lambda i: (last_tile, 0))]
        + [whole(a) for a in (tokens, own, near, near_weight)],
        out_specs=[WHOLE, whole(tokens)],
        scratch_shapes=[pltpu.VMEM(weight_far.shape, BF16), pltpu.SemaphoreType.DMA((2,))],
        compiler_params=pltpu.CompilerParams(vmem_limit_bytes=VMEM_LIMIT),
        cost_estimate=pl.CostEstimate(flops=0, bytes_accessed=0, transcendentals=0),
    )(start, vocab, weight_far, vocab, tokens, own, near, near_weight)


def rows_body(gain_far, base, far, last, far_weight, last_weight, *refs):
    squares, scaled, again, gain, sem = refs[-5:]
    copy = pltpu.make_async_copy(gain_far, gain, sem.at[0])
    copy.start()
    rows = base[...] + mm(far_weight[...], far[...]).astype(BF16).astype(F32)
    rows = rows + mm(last_weight[...], last[...]).astype(BF16).astype(F32)
    squares[...] = jnp.sum(rows * rows, axis=0, keepdims=True)
    copy.wait()
    scaled[...] = (rows * (gain[...] * SHRINK)).astype(BF16)
    again[...] = scaled[...]


def held_body(limit, start, half, scaled, out):
    row = start[0] + lax.broadcasted_iota(jnp.int32, out.shape, 0)
    out[...] = jnp.where(row < limit, mm(half[...], scaled[...]), NEG).astype(BF16)


def logits_body(limit, start, vocab, scaled, *refs):
    out = refs[-1]
    first = (start[0] + pl.program_id(0)) * out.shape[0]
    row = first + lax.broadcasted_iota(jnp.int32, out.shape, 0)
    out[...] = jnp.where(row < limit, mm(vocab[...], scaled[...]), NEG).astype(BF16)


def half_logits(start, vocab, scaled, after=()):
    limit, width = vocab.shape
    count = scaled.shape[1]
    tile = pl.cdiv(limit, 4 * 32) * 32
    return pl.pallas_call(
        partial(logits_body, limit),
        grid_spec=pltpu.PrefetchScalarGridSpec(
            num_scalar_prefetch=1,
            grid=(2,),
            in_specs=[
                pl.BlockSpec((tile, width), lambda i, start: (start[0] + i, 0)),
                pl.BlockSpec((width, count), lambda i, start: (0, 0)),
            ]
            + [ANYWHERE] * len(after),
            out_specs=pl.BlockSpec((tile, count), lambda i, start: (i, 0)),
        ),
        out_shape=struct((2 * tile, count), BF16),
        compiler_params=pltpu.CompilerParams(vmem_limit_bytes=VMEM_LIMIT),
        cost_estimate=pl.CostEstimate(flops=0, bytes_accessed=0, transcendentals=0),
    )(start, vocab, scaled, *after)


def fold_body(side, kept, came, send, keep):
    quarter = send.shape[0]
    for out, turn in ((send, 1 - side[0]), (keep, side[0])):
        at = pl.ds(pl.multiple_of(turn * quarter, 16), quarter)
        out[...] = (kept[at, :].astype(F32) + came[at, :].astype(F32)).astype(out.dtype)


def top_body(kept, came, *refs):
    out = refs[-1]
    out[...] = jnp.max(kept[...] + came[...].astype(F32), axis=0, keepdims=True)


def pair_body(first, second, *refs):
    refs[-1][0:1, :] = first[...]
    refs[-1][1:2, :] = second[...]


def split_columns(mine, source, outs):
    width = outs[0].shape[0]
    for b in range(4):
        at = pl.ds(pl.multiple_of((mine[0] ^ b) * width, width), width)
        outs[b][...] = source[:, at].T


def shards(
    tokens,
    norm_gain,
    w_query,
    w_key,
    w_value,
    w_out,
    final_gain,
    w_vocab,
    segment_ids,
    prompt_lengths,
    request_slots,
):
    rows, columns = tokens.shape
    half = rows // 2
    width = w_query.shape[1]
    heads = width // HD
    n_seq = lax.axis_size("seq")
    span = n_seq // 4
    seq_index = lax.axis_index("seq")
    tp_index = lax.axis_index("tp")
    mine = tp_index.reshape(1)
    base = seq_index * rows
    requests = request_slots.shape[0]
    prompts = prompt_lengths.shape[0]

    far = swap(tokens, "tp", 2)
    pieces = [tokens, swap(tokens, "tp", 1), far]
    gain = norm_gain.reshape(4, columns)
    weights = [
        pltpu.with_memory_space_constraint(w, pltpu.HBM) for w in (w_key, w_value, w_query)
    ]
    *sums, w_split, w_1, w_2, w_3, far_weights, last_kv, last_query = project(
        (0, 1), mine, gain, pieces[:2], weights, w_out=w_out
    )
    w_parts = [w_split] + [swap(w, "tp", b) for b, w in ((1, w_1), (2, w_2), (3, w_3))]
    powers = np.arange(HD // 2, dtype=np.float32) * np.float32(2.0 / HD)
    inverse = (np.float32(10000.0) ** -powers).astype(np.float32)[:, None]
    cosine, sine, low, request_low = call(
        prepare_body,
        [
            struct((HD // 2, rows), F32),
            struct((HD // 2, rows), F32),
            struct((1, rows), jnp.int32),
            struct((1, requests), jnp.int32),
        ],
        [base.reshape(1), prompt_lengths],
        pinned([segment_ids[None, :], jnp.asarray(inverse)]),
        sums[1:2],
        blocked=True,
    )
    last_gain = final_gain[:, None]
    relayed, far = call(
        twice_body, [struct(far.shape, BF16)] * 2, [], [far], (sums[1], cosine, last_gain)
    )
    pieces = pieces[:2] + [far, swap(relayed, "tp", 1)]

    asked = request_slots[None, :]
    inside = asked - base
    (own_tokens,) = call(
        pick_body, [struct((columns, requests), BF16)], [base.reshape(1)], pinned([asked, tokens]),
        blocked=True,
    )
    all_tokens = [own_tokens]
    *kv_sums, query_sums, query_squares = project(
        (2,), mine, gain, pieces[2:3], [far_weights], sums, None, (), length=10
    )
    ending = (base.reshape(1), cosine, sine, asked)
    query, own_query = project(
        (3,), mine, gain, pieces[3:], [last_query], (query_sums, query_squares), ending, (), 2, (2,)
    )
    asking = [own_query] + [shifted(own_query, "seq", -by) for by in range(1, span + 1)]
    bit = n_seq // 2
    while bit:
        all_tokens += call(
            add_body,
            [struct(own_tokens.shape, BF16)],
            [],
            [all_tokens[-1], swap(all_tokens[-1], "seq", bit)],
            sums[1:2] if len(all_tokens) == 1 else (own_query,),
        )
        bit //= 2
    asked_kv, own_kv, kv, kv_half = project(
        (3,),
        mine,
        gain,
        pieces[3:],
        [last_kv],
        kv_sums,
        ending,
        (own_query,),
        10,
        (0, 1),
    )

    kv_cache = jnp.transpose(kv.reshape(heads, 2 * HD, rows), (0, 2, 1))
    behind = shifted(kv, "seq", 1)

    last_start = n_seq - span - 1
    ends = jnp.cumsum(prompt_lengths)
    reach = (ends - 1) // rows - (ends - prompt_lengths) // rows
    longest = jnp.max(jnp.where(jnp.arange(prompts) < prompts - 1, reach, 0))
    sources = [(0, 0, n_seq, 0), (1, 0, n_seq, 0)]
    blocks = [own_kv, behind]
    for by in range(2, span + 1):
        early = [(i, i + by) for i in range(last_start + 1 - by)]
        late = [(i, i + by) for i in range(last_start, n_seq - by)]
        sources.append((by, 0, last_start, 0))
        blocks.append(
            lax.cond(
                longest >= by,
                lambda array, pairs=early: lax.ppermute(array, "seq", pairs),
                jnp.zeros_like,
                kv,
            )
        )
        from_half = 1 if by == span else 0
        sources.append((by, last_start + by, n_seq, from_half))
        blocks.append(lax.ppermute(kv_half if from_half else kv, "seq", late))
    halo = tuple(blocks[2:4])

    (mixed,) = call(
        partial(request_body, len(asking)),
        [struct((width + LEVEL_ROWS, requests), BF16)],
        [],
        [request_low, inside, asked_kv, *asking],
        all_tokens[2:3],
        length=10,
    )
    afters = [
        w_parts[2:3] + pinned(halo[1:]),
        halo[:1] + tuple(all_tokens[3:4]),
        w_parts[3:4] + [all_tokens[-1]],
    ]
    bit = 1
    while bit < n_seq:
        flip = ((seq_index & bit) > 0).astype(jnp.int32).reshape(1)
        after = afters.pop(0) if afters else ()
        other = swap(mixed, "seq", bit)
        bit *= 2
        kept_rows = width + LEVEL_ROWS if bit < n_seq else width
        mixed = combine(flip, mixed, other, kept_rows, after)
    _, near_mixed, far_mixed, last_mixed = spread(mixed)

    core = tp_index & 1
    side = tp_index >> 1
    vocab = pltpu.with_memory_space_constraint(w_vocab.T, pltpu.HBM)
    limit = vocab.shape[0]
    vocab_rows = pl.cdiv(limit, 4 * 32) * 64
    away = (vocab_rows * (1 - core)).reshape(1)
    far_gain, own_weight = pinned([last_gain, w_split])
    held, field = begin_rows(
        away, vocab, own_weight, all_tokens[-1], mixed, near_mixed, w_parts[1]
    )
    squares, scaled, again = call(
        rows_body,
        [struct((1, requests), F32)] + [struct(own_tokens.shape, BF16)] * 2,
        [],
        [field, far_mixed, last_mixed, *w_parts[2:]],
        scratch=[pltpu.VMEM((columns, 1), F32), pltpu.SemaphoreType.DMA((1,))],
        far=[far_gain],
    )
    (sent,) = call(
        partial(held_body, limit),
        [struct((vocab_rows, requests), BF16)],
        [away],
        [held, scaled],
    )
    kept = half_logits((2 * core).reshape(1), vocab, again, (sent,))
    quarter = kept.shape[0] // 2
    sent, kept = call(
        fold_body,
        [struct((quarter, requests), BF16), struct((quarter, requests), F32)],
        [side.reshape(1)],
        [kept, swap(sent, "tp", 1)],
    )
    state = ()
    while sources:
        last = len(sources) <= 4
        state = attend(
            sources[:4], last, seq_index.reshape(1), low, query, blocks[:4], state, 30
        )
        sources, blocks = sources[4:], blocks[4:]
    (best,) = call(
        top_body, [struct((1, requests), F32)], [], [kept, swap(sent, "tp", 2)], state[:1]
    )
    bit = 1
    while bit < n_seq:
        best = jnp.maximum(best, swap(best, "seq", bit))
        bit *= 2
    attended = spread(state[0])
    (pair,) = call(
        pair_body, [struct((2, requests), F32)], [], [best, squares], attended[2:3]
    )
    for bit in (2, 1):
        other = swap(pair, "tp", bit)
        pair = jnp.stack([jnp.maximum(pair[0], other[0]), pair[1] + other[1]])
    hidden_norm = jnp.sqrt(pair[1] / D + EPS)
    top_logit = pair[0] / hidden_norm * (1.0 / SHRINK)

    summed = sum(
        mm_last(part, w).astype(BF16).astype(F32) for part, w in zip(attended, w_parts)
    )
    hidden = (tokens.astype(F32) + summed).astype(BF16)
    return (kv_cache, hidden, hidden_norm, top_logit)


def solution(mesh):
    return jax.shard_map(
        shards,
        mesh=mesh,
        in_specs=(
            P("seq", "tp"),
            P(),
            P(None, "tp"),
            P(None, "tp"),
            P(None, "tp"),
            P("tp", None),
            P("tp"),
            P("tp", "seq"),
            P("seq"),
            P(),
            P(),
        ),
        out_specs=(P("tp", "seq", None), P("seq", "tp"), P(), P()),
        check_vma=False,
    )
```

```python
from functools import partial

import jax
import jax.numpy as jnp
import numpy as np
from jax import lax
from jax.experimental import pallas as pl
from jax.experimental.pallas import tpu as pltpu
from jax.sharding import PartitionSpec as P

D = 3072
HD = 96
EPS = 1e-05
NEG = -1e30
FLOOR = -5e29
NEVER = 2**30
LEVEL_ROWS = 16
SHRINK = 2.0**-16
DAMP = 2.0**-24
LOG2_E = 1.4426950408889634
F32 = jnp.float32
BF16 = jnp.bfloat16
VMEM_LIMIT = 12 * 1024 * 1024

SCALARS = pl.BlockSpec(memory_space=pltpu.SMEM)
ANYWHERE = pl.BlockSpec(memory_space=pl.ANY)
FAR_MEMORY = pl.BlockSpec(memory_space=pltpu.HBM)


WHOLE = pl.BlockSpec(memory_space=pltpu.VMEM)


def whole(array):
    return pl.BlockSpec(array.shape, lambda i: (0, 0), pipeline_mode=pl.Buffered(1))


def call(body, outs, scalars, arrays, after=(), scratch=(), length=0, far=(), blocked=False):
    return pl.pallas_call(
        body,
        grid=(1,) if blocked else (),
        out_shape=outs,
        in_specs=[SCALARS] * len(scalars)
        + [FAR_MEMORY] * len(far)
        + [whole(array) if blocked else WHOLE for array in arrays]
        + [ANYWHERE] * len(after),
        out_specs=[whole(out) if blocked else WHOLE for out in outs],
        scratch_shapes=list(scratch),
        compiler_params=pltpu.CompilerParams(vmem_limit_bytes=VMEM_LIMIT),
        cost_estimate=pl.CostEstimate(
            flops=length * 10**9, bytes_accessed=0, transcendentals=0
        ),
    )(*scalars, *far, *arrays, *after)


def pinned(arrays):
    return [pltpu.with_memory_space_constraint(a, pltpu.HBM) for a in arrays]


def struct(shape, dtype):
    return jax.ShapeDtypeStruct(shape, dtype)


def swap(array, axis, bit):
    count = lax.axis_size(axis)
    return lax.ppermute(array, axis, [(i, i ^ bit) for i in range(count)])


def shifted(array, axis, by):
    count = lax.axis_size(axis)
    pairs = [(i, i + by) for i in range(count) if 0 <= i + by < count]
    return lax.ppermute(array, axis, pairs)


def spread(array):
    far = swap(array, "tp", 2)
    near = swap(array, "tp", 1)
    return array, near, far, swap(far, "tp", 1)


def mm(a, b):
    return jnp.dot(a, b, preferred_element_type=F32)


def mm_last(a, b):
    return lax.dot_general(a, b, (((1,), (1,)), ((), ())), preferred_element_type=F32)


def mm_first(a, b):
    return lax.dot_general(a, b, (((0,), (0,)), ((), ())), preferred_element_type=F32)


AHEAD = ((2, (0, 1, 2)), (3, (0, 1)), (3, (2,)))


def project_body(blocks, first, last, kinds, *refs):
    refs = list(refs)
    take = lambda count: [refs.pop(0) for _ in range(count)]
    mine = refs.pop(0)
    base = refs.pop(0) if last else None
    weights = take(3 if first else 1)
    (gain,) = take(1)
    pieces = take(len(blocks))
    accum, squares = take(2) if not first else (None, None)
    cosine, sine, asked = take(3) if last else (None, None, None)
    if first:
        held, sems = refs[-2:]
        del refs[-2:]
    rows, part = pieces[0].shape
    width = weights[0].shape[-1]
    copies = []
    onward = []
    if first:
        split_columns(mine, refs.pop(0), refs[-7:-3])
        for (block, needed), out in zip(AHEAD, refs[-3:]):
            at = pl.ds(pl.multiple_of((mine[0] ^ block) * part, part), part)
            onward += [
                pltpu.make_async_copy(weights[i].at[at, :], out.at[j], sems.at[i, block])
                for j, i in enumerate(needed)
            ]
        del refs[-7:]
    for i in range(3 if first else 0):
        for j, block in enumerate(blocks):
            at = pl.ds(pl.multiple_of((mine[0] ^ block) * part, part), part)
            copies.append(
                pltpu.make_async_copy(weights[i].at[at, :], held.at[i, j], sems.at[i, j])
            )
    for copy in copies + onward:
        copy.start()
    wide = [piece[...].astype(F32) for piece in pieces]
    total = sum(jnp.sum(w * w, axis=1, keepdims=True) for w in wide)
    if not first:
        total = total + squares[...]
    scaled = [
        (w * (gain[pl.ds(mine[0] ^ block, 1), :] * DAMP)).astype(BF16)
        for block, w in zip(blocks, wide)
    ]
    factor = lax.rsqrt(total / D + EPS) * (1.0 / DAMP)
    middle = HD // 2
    for i in kinds:
        place = kinds.index(i)
        at = slice(place * width, (place + 1) * width)
        field = 0.0
        for j, x in enumerate(scaled):
            if first:
                copies[i * len(blocks) + j].wait()
                field = field + mm(x, held[i, j])
            else:
                field = field + mm(x, weights[0][place])
        if not first:
            field = field + accum[:, at]
        if first:
            refs[-2][:, at] = field
            continue
        if not last:
            out = refs[-4] if i < 2 else refs[-2]
            out[:, at if i < 2 else slice(0, width)] = field
            continue
        field = (field * factor).T
        if 2 in kinds:
            query, own = refs[-2:]
        else:
            kv = refs[-4]
        for h in range(width // HD):
            at = h * HD
            a = field[at : at + middle]
            b = field[at + middle : at + HD]
            if i == 1:
                kv[2 * at + HD : 2 * at + 2 * HD, :] = field[at : at + HD].astype(BF16)
            else:
                to, out = (at, query) if i == 2 else (2 * at, kv)
                out[to : to + middle, :] = (a * cosine[...] - b * sine[...]).astype(BF16)
                out[to + middle : to + HD, :] = (b * cosine[...] + a * sine[...]).astype(BF16)
    if last and 2 not in kinds:
        refs[-3][...] = kv[...]
        refs[-2][...] = kv[...]
        refs[-1][...] = kv[:, rows // 2 :]
    if last and 2 in kinds:
        row = base[0] + lax.broadcasted_iota(jnp.int32, (rows, asked.shape[1]), 0)
        own[...] = mm(query[...], (asked[...] == row).astype(BF16)).astype(BF16)
    if not last:
        refs[-1][...] = total
        if not first:
            refs[-3][...] = total
    for copy in onward:
        copy.wait()


def project(
    blocks,
    mine,
    gain,
    pieces,
    weights,
    before=(),
    ending=None,
    after=(),
    length=0,
    kinds=(0, 1, 2),
    w_out=None,
):
    rows = pieces[0].shape[0]
    width = weights[0].shape[-1]
    scalars, arrays = [mine], [gain, *pieces, *before]
    if ending is None:
        outs = [struct((rows, 3 * width), F32), struct((rows, 1), F32)]
        if before:
            outs = [struct((rows, 2 * width), F32), struct((rows, 1), F32)]
            outs += [struct((rows, width), F32), struct((rows, 1), F32)]
    if not before:
        arrays.append(w_out)
        outs += [struct((w_out.shape[1] // 4, w_out.shape[0]), BF16)] * 4
        outs += [struct((len(n), pieces[0].shape[1], width), BF16) for _, n in AHEAD]
    if ending is not None:
        base, cosine, sine, asked = ending
        scalars.append(base)
        arrays += [cosine, sine, asked]
        outs = [struct((2 * width, rows), BF16)] * 3 + [struct((2 * width, rows // 2), BF16)]
        if 2 in kinds:
            outs = [struct((width, rows), BF16), struct((width, asked.shape[1]), BF16)]
    body = partial(project_body, blocks, not before, ending is not None, kinds)
    if before:
        arrays = list(weights) + arrays
        return call(body, outs, scalars, arrays, after, length=length)
    scratch = [
        pltpu.VMEM((3, len(blocks), pieces[0].shape[1], width), BF16),
        pltpu.SemaphoreType.DMA((3, 4)),
    ]
    return call(body, outs, scalars, arrays, after, scratch, length, weights)


def copy_body(source, *refs):
    refs[-1][...] = source[...]


def twice_body(source, *refs):
    refs[-2][...] = source[...]
    refs[-1][...] = source[...]


def prepare_body(base, lengths, segments, inverse, *refs):
    cosine, sine, low, asked_low = refs[-4:]
    prompts = lengths.shape[0]
    rows = segments.shape[1]
    segment = segments[...]
    asked = lax.broadcasted_iota(jnp.int32, asked_low.shape, 1)
    each = asked_low.shape[1] // prompts
    first = jnp.zeros((1, rows), jnp.int32)
    asked_first = jnp.zeros(asked_low.shape, jnp.int32)
    start = jnp.int32(0)
    for p in range(prompts):
        first = jnp.where(segment == p, start, first)
        asked_first = jnp.where(
            (asked >= p * each) & (asked < (p + 1) * each), start, asked_first
        )
        start = start + lengths[p]
    valid = segment >= 0
    slot = base[0] + lax.broadcasted_iota(jnp.int32, (1, rows), 1)
    position = jnp.where(valid, slot - first, 0).astype(F32)
    angles = inverse[...] * position
    cosine[...] = jnp.cos(angles)
    sine[...] = jnp.sin(angles)
    low[...] = jnp.where(valid, first - base[0], NEVER)
    asked_low[...] = asked_first - base[0]


def pick_body(base, slots, tokens, out):
    rows = tokens.shape[0]
    count = slots.shape[1]
    row = base[0] + lax.broadcasted_iota(jnp.int32, (rows, count), 0)
    out[...] = mm_first(tokens[...], (slots[...] == row).astype(BF16)).astype(BF16)


def add_body(first, second, *refs):
    refs[-1][...] = first[...] + second[...]


def request_body(count, low, high, block, *refs):
    query = sum(part[...] for part in refs[:count])
    width, rows = query.shape
    half = block.shape[1] // 2
    allowed = []
    for i in range(2):
        key_slot = i * half + lax.broadcasted_iota(jnp.int32, (half, rows), 0)
        allowed.append((key_slot >= low[...]) & (key_slot <= high[...]))
    results = []
    levels = []
    for h in range(width // HD):
        at = slice(h * HD, (h + 1) * HD)
        k_at = slice(2 * h * HD, (2 * h + 1) * HD)
        v_at = slice((2 * h + 1) * HD, (2 * h + 2) * HD)
        scores = [
            jnp.where(
                allowed[i], mm_first(block[k_at, i * half : (i + 1) * half], query[at, :]) * HD**-0.5, NEG
            )
            for i in range(2)
        ]
        largest = jnp.maximum(*[jnp.max(part, axis=0, keepdims=True) for part in scores])
        largest = jnp.maximum(largest, FLOOR)
        weights = [jnp.exp(part - largest) for part in scores]
        total = sum(jnp.sum(part, axis=0, keepdims=True) for part in weights)
        mixed = sum(
            mm(block[v_at, i * half : (i + 1) * half], weights[i].astype(BF16)) for i in range(2)
        )
        filled = total > 0
        safe = jnp.where(filled, total, 1.0)
        results.append((mixed * (1.0 / safe)).astype(BF16))
        levels.append(jnp.where(filled, largest + jnp.log(safe), NEG))
    out = refs[-1]
    for h, result in enumerate(results):
        out[h * HD : (h + 1) * HD, :] = result
    out[width:, :] = pack_levels(levels)


def pack_levels(levels):
    row = lax.broadcasted_iota(jnp.int32, (LEVEL_ROWS, levels[0].shape[1]), 0)
    packed = jnp.zeros(row.shape, F32)
    for h, level in enumerate(levels):
        for part in range(3):
            rounded = level.astype(BF16).astype(F32)
            packed = jnp.where(row == 3 * h + part, rounded, packed)
            level = level - rounded
    return packed.astype(BF16)


def combine_body(flip, own, other, *refs):
    width = own.shape[0] - LEVEL_ROWS
    turned = flip[0] > 0
    a = own[...].astype(F32)
    b = other[...].astype(F32)
    lower = jnp.where(turned, b, a)
    upper = jnp.where(turned, a, b)
    levels = []
    results = []
    for h in range(width // HD):
        marks = []
        for side in (lower, upper):
            at = width + 3 * h
            marks.append(side[at : at + 1] + side[at + 1 : at + 2] + side[at + 2 : at + 3])
        top = jnp.maximum(*marks)
        one, two = (jnp.exp(mark - top) for mark in marks)
        both = one + two
        levels.append(top + jnp.log(both))
        at = slice(h * HD, (h + 1) * HD)
        results.append((lower[at] * (one / both) + upper[at] * (two / both)).astype(BF16))
    out = refs[-1]
    for h, result in enumerate(results):
        out[h * HD : (h + 1) * HD, :] = result
    if out.shape[0] > width:
        out[width:, :] = pack_levels(levels)


def combine(flip, own, other, rows, after=()):
    return call(
        combine_body,
        [struct((rows, own.shape[1]), BF16)],
        [flip],
        [own, other],
        after,
        length=3,
        blocked=True,
    )[0]


def attend_body(sources, last, place, low, query, *refs):
    width, rows = query.shape
    half = rows // 2
    heads = width // HD
    blocks = refs[: len(sources)]
    state = refs[len(sources) :]
    accum, largest, total = refs[-3:]
    if sources[0][0] == 0:
        accum[...] = jnp.zeros(accum.shape, F32)
        largest[...] = jnp.full(largest.shape, FLOOR, F32)
        total[...] = jnp.zeros(total.shape, F32)
    else:
        accum[...] = state[0][...]
        largest[...] = state[1][...]
        total[...] = state[2][...]

    def visit(distance, block, part, i, until, j):
        q_at = slice(i * half, until * half)
        k_half = slice(part * half, (part + 1) * half)
        shape = (half, (until - i) * half)
        key_slot = (
            j * half - distance * rows + lax.broadcasted_iota(jnp.int32, shape, 0)
        )
        allowed = key_slot >= low[:, q_at]
        if distance == 0:
            query_slot = i * half + lax.broadcasted_iota(jnp.int32, shape, 1)
            allowed = allowed & (key_slot <= query_slot)
        scores = [
            mm_first(
                block[2 * h * HD : (2 * h + 1) * HD, k_half],
                query[h * HD : (h + 1) * HD, q_at],
            )
            for h in range(heads)
        ]
        parts = []
        for h in range(heads):
            score = jnp.where(allowed, scores[h] * (HD**-0.5 * LOG2_E), NEG)
            m_old = largest[h : h + 1, q_at]
            m_new = jnp.maximum(m_old, jnp.max(score, axis=0, keepdims=True))
            parts.append((m_new, jnp.exp2(score - m_new), jnp.exp2(m_old - m_new)))
        done = []
        for h, (m_new, weights, factor) in enumerate(parts):
            v_at = slice((2 * h + 1) * HD, (2 * h + 2) * HD)
            t_new = total[h : h + 1, q_at] * factor + jnp.sum(weights, axis=0, keepdims=True)
            mixed = accum[h * HD : (h + 1) * HD, q_at] * factor + mm(
                block[v_at, k_half], weights.astype(BF16)
            )
            done.append((m_new, t_new, mixed))
        for h, (m_new, t_new, mixed) in enumerate(done):
            accum[h * HD : (h + 1) * HD, q_at] = mixed
            largest[h : h + 1, q_at] = m_new
            total[h : h + 1, q_at] = t_new

    limits = [jnp.min(low[:, i * half : (i + 1) * half]) for i in range(2)]
    for (distance, least, most, skipped), block in zip(sources, blocks):
        here = (place[0] >= least) & (place[0] <= most)
        for j in range(skipped, 2):
            end = (j + 1) * half - distance * rows
            look = partial(visit, distance, block, j - skipped)
            if distance == 0 and j == 1:
                pl.when(limits[1] < end)(partial(look, 1, 2, j))
            else:
                pl.when(here & (limits[1] < end))(partial(look, 0, 2, j))
                pl.when(here & (limits[1] >= end) & (limits[0] < end))(partial(look, 0, 1, j))
    if last:
        out = refs[-4]
        for h in range(heads):
            at = slice(h * HD, (h + 1) * HD)
            t_h = total[h : h + 1, :]
            accum[at, :] = accum[at, :] * (1.0 / jnp.where(t_h > 0, t_h, 1.0))
        out[...] = accum[...].T.astype(BF16)


def attend(sources, last, place, low, query, blocks, state, length=0, after=()):
    width, rows = query.shape
    shapes = [struct((width, rows), F32), struct((8, rows), F32), struct((8, rows), F32)]
    scratch = []
    outs = shapes
    if last:
        scratch = [pltpu.VMEM(s.shape, s.dtype) for s in shapes]
        outs = [struct((rows, width), BF16)]
    return call(
        partial(attend_body, sources, last),
        outs,
        [place],
        [low, query, *blocks, *state],
        after,
        scratch,
        length,
        blocked=True,
    )


def begin_body(limit, start, vocab, weight_far, tail, tokens, own, near, near_weight, *refs):
    half, base, weight, sems = refs[-4:]
    rows = half.shape[0]
    whole_rows = (limit - rows) // 16 * 16
    lower = start[0] == 0

    def fetch(at, count):
        return pltpu.make_async_copy(
            vocab.at[pl.ds(at, count), :], half.at[pl.ds(0, count), :], sems.at[0]
        )

    load = pltpu.make_async_copy(weight_far, weight, sems.at[1])
    load.start()

    @pl.when(lower)
    def _():
        fetch(0, rows).start()

    @pl.when(jnp.logical_not(lower))
    def _():
        fetch(rows, whole_rows).start()

    field = tokens[...].astype(F32) + mm(near_weight[...], near[...]).astype(BF16).astype(F32)
    load.wait()
    base[...] = field + mm(weight[...], own[...]).astype(BF16).astype(F32)

    @pl.when(lower)
    def _():
        fetch(0, rows).wait()

    @pl.when(jnp.logical_not(lower))
    def _():
        fetch(rows, whole_rows).wait()
        if limit > rows + whole_rows:
            half[whole_rows : whole_rows + 16, :] = tail[...]


def begin_rows(start, vocab, weight_far, tokens, own, near, near_weight):
    limit, width = vocab.shape
    count = tokens.shape[1]
    rows = pl.cdiv(limit, 4 * 32) * 64
    last_tile = (limit - 1) // 16
    return pl.pallas_call(
        partial(begin_body, limit),
        grid=(1,),
        out_shape=[struct((rows, width), BF16), struct((width, count), F32)],
        in_specs=[SCALARS, FAR_MEMORY, FAR_MEMORY]
        + [pl.BlockSpec((16, width), lambda i: (last_tile, 0))]
        + [whole(a) for a in (tokens, own, near, near_weight)],
        out_specs=[WHOLE, whole(tokens)],
        scratch_shapes=[pltpu.VMEM(weight_far.shape, BF16), pltpu.SemaphoreType.DMA((2,))],
        compiler_params=pltpu.CompilerParams(vmem_limit_bytes=VMEM_LIMIT),
        cost_estimate=pl.CostEstimate(flops=0, bytes_accessed=0, transcendentals=0),
    )(start, vocab, weight_far, vocab, tokens, own, near, near_weight)


def rows_body(gain_far, base, far, last, far_weight, last_weight, *refs):
    squares, scaled, again, gain, sem = refs[-5:]
    copy = pltpu.make_async_copy(gain_far, gain, sem.at[0])
    copy.start()
    rows = base[...] + mm(far_weight[...], far[...]).astype(BF16).astype(F32)
    rows = rows + mm(last_weight[...], last[...]).astype(BF16).astype(F32)
    squares[...] = jnp.sum(rows * rows, axis=0, keepdims=True)
    copy.wait()
    scaled[...] = (rows * (gain[...] * SHRINK)).astype(BF16)
    again[...] = scaled[...]


def held_body(limit, start, half, scaled, out):
    row = start[0] + lax.broadcasted_iota(jnp.int32, out.shape, 0)
    out[...] = jnp.where(row < limit, mm(half[...], scaled[...]), NEG).astype(BF16)


def logits_body(limit, start, vocab, scaled, *refs):
    out = refs[-1]
    first = (start[0] + pl.program_id(0)) * out.shape[0]
    row = first + lax.broadcasted_iota(jnp.int32, out.shape, 0)
    out[...] = jnp.where(row < limit, mm(vocab[...], scaled[...]), NEG).astype(BF16)


def half_logits(start, vocab, scaled, after=()):
    limit, width = vocab.shape
    count = scaled.shape[1]
    tile = pl.cdiv(limit, 4 * 32) * 32
    return pl.pallas_call(
        partial(logits_body, limit),
        grid_spec=pltpu.PrefetchScalarGridSpec(
            num_scalar_prefetch=1,
            grid=(2,),
            in_specs=[
                pl.BlockSpec((tile, width), lambda i, start: (start[0] + i, 0)),
                pl.BlockSpec((width, count), lambda i, start: (0, 0)),
            ]
            + [ANYWHERE] * len(after),
            out_specs=pl.BlockSpec((tile, count), lambda i, start: (i, 0)),
        ),
        out_shape=struct((2 * tile, count), BF16),
        compiler_params=pltpu.CompilerParams(vmem_limit_bytes=VMEM_LIMIT),
        cost_estimate=pl.CostEstimate(flops=0, bytes_accessed=0, transcendentals=0),
    )(start, vocab, scaled, *after)


def fold_body(side, kept, came, send, keep):
    quarter = send.shape[0]
    for out, turn in ((send, 1 - side[0]), (keep, side[0])):
        at = pl.ds(pl.multiple_of(turn * quarter, 16), quarter)
        out[...] = (kept[at, :].astype(F32) + came[at, :].astype(F32)).astype(out.dtype)


def top_body(kept, came, *refs):
    out = refs[-1]
    out[...] = jnp.max(kept[...] + came[...].astype(F32), axis=0, keepdims=True)


def join_body(pair, other, *refs):
    refs[-1][0:1, :] = jnp.maximum(pair[0:1, :], other[0:1, :])
    refs[-1][1:2, :] = pair[1:2, :] + other[1:2, :]


def pair_body(first, second, *refs):
    refs[-1][0:1, :] = first[...]
    refs[-1][1:2, :] = second[...]


def split_columns(mine, source, outs):
    width = outs[0].shape[0]
    for b in range(4):
        at = pl.ds(pl.multiple_of((mine[0] ^ b) * width, width), width)
        outs[b][...] = source[:, at].T


def shards(
    tokens,
    norm_gain,
    w_query,
    w_key,
    w_value,
    w_out,
    final_gain,
    w_vocab,
    segment_ids,
    prompt_lengths,
    request_slots,
):
    rows, columns = tokens.shape
    half = rows // 2
    width = w_query.shape[1]
    heads = width // HD
    n_seq = lax.axis_size("seq")
    span = n_seq // 4
    seq_index = lax.axis_index("seq")
    tp_index = lax.axis_index("tp")
    mine = tp_index.reshape(1)
    base = seq_index * rows
    requests = request_slots.shape[0]
    prompts = prompt_lengths.shape[0]

    far = swap(tokens, "tp", 2)
    pieces = [tokens, swap(tokens, "tp", 1), far]
    gain = norm_gain.reshape(4, columns)
    weights = [
        pltpu.with_memory_space_constraint(w, pltpu.HBM) for w in (w_key, w_value, w_query)
    ]
    *sums, w_split, w_1, w_2, w_3, far_weights, last_kv, last_query = project(
        (0, 1), mine, gain, pieces[:2], weights, w_out=w_out
    )
    w_parts = [w_split] + [swap(w, "tp", b) for b, w in ((1, w_1), (2, w_2), (3, w_3))]
    powers = np.arange(HD // 2, dtype=np.float32) * np.float32(2.0 / HD)
    inverse = (np.float32(10000.0) ** -powers).astype(np.float32)[:, None]
    cosine, sine, low, request_low = call(
        prepare_body,
        [
            struct((HD // 2, rows), F32),
            struct((HD // 2, rows), F32),
            struct((1, rows), jnp.int32),
            struct((1, requests), jnp.int32),
        ],
        [base.reshape(1), prompt_lengths],
        pinned([segment_ids[None, :], jnp.asarray(inverse)]),
        sums[1:2],
        blocked=True,
    )
    last_gain = final_gain[:, None]
    asked = request_slots[None, :]
    inside = asked - base
    (own_tokens,) = call(
        pick_body, [struct((columns, requests), BF16)], [base.reshape(1)], pinned([asked, tokens]),
        blocked=True,
    )
    all_tokens = [own_tokens]
    all_tokens += call(
        add_body,
        [struct(own_tokens.shape, BF16)],
        [],
        [own_tokens, swap(own_tokens, "seq", n_seq // 2)],
        sums[1:2],
    )
    relayed, far = call(
        twice_body, [struct(far.shape, BF16)] * 2, [], [far], (sums[1], cosine, last_gain, all_tokens[1])
    )
    pieces = pieces[:2] + [far, swap(relayed, "tp", 1)]

    *kv_sums, query_sums, query_squares = project(
        (2,), mine, gain, pieces[2:3], [far_weights], sums, None, (), length=4
    )
    ending = (base.reshape(1), cosine, sine, asked)
    query, own_query = project(
        (3,), mine, gain, pieces[3:], [last_query], (query_sums, query_squares), ending, (), 2, (2,)
    )
    asking = [own_query] + [shifted(own_query, "seq", -by) for by in range(1, span + 1)]
    bit = n_seq // 4
    while bit:
        all_tokens += call(
            add_body,
            [struct(own_tokens.shape, BF16)],
            [],
            [all_tokens[-1], swap(all_tokens[-1], "seq", bit)],
            (own_query,),
        )
        bit //= 2
    asked_kv, own_kv, kv, kv_half = project(
        (3,),
        mine,
        gain,
        pieces[3:],
        [last_kv],
        kv_sums,
        ending,
        (own_query,),
        10,
        (0, 1),
    )

    kv_cache = jnp.transpose(kv.reshape(heads, 2 * HD, rows), (0, 2, 1))
    behind = shifted(kv, "seq", 1)

    last_start = n_seq - span - 1
    ends = jnp.cumsum(prompt_lengths)
    reach = (ends - 1) // rows - (ends - prompt_lengths) // rows
    longest = jnp.max(jnp.where(jnp.arange(prompts) < prompts - 1, reach, 0))
    sources = [(0, 0, n_seq, 0), (1, 0, n_seq, 0)]
    blocks = [own_kv, behind]
    for by in range(2, span + 1):
        early = [(i, i + by) for i in range(last_start + 1 - by)]
        late = [(i, i + by) for i in range(last_start, n_seq - by)]
        sources.append((by, 0, last_start, 0))
        blocks.append(
            lax.cond(
                longest >= by,
                lambda array, pairs=early: lax.ppermute(array, "seq", pairs),
                jnp.zeros_like,
                kv,
            )
        )
        from_half = 1 if by == span else 0
        sources.append((by, last_start + by, n_seq, from_half))
        blocks.append(lax.ppermute(kv_half if from_half else kv, "seq", late))
    halo = tuple(blocks[2:4])

    (mixed,) = call(
        partial(request_body, len(asking)),
        [struct((width + LEVEL_ROWS, requests), BF16)],
        [],
        [request_low, inside, asked_kv, *asking],
        all_tokens[2:3],
        length=10,
    )
    afters = [
        w_parts[2:3] + pinned(halo[1:]),
        halo[:1] + tuple(all_tokens[3:4]),
        w_parts[3:4] + [all_tokens[-1]],
    ]
    bit = 1
    while bit < n_seq:
        flip = ((seq_index & bit) > 0).astype(jnp.int32).reshape(1)
        after = afters.pop(0) if afters else ()
        other = swap(mixed, "seq", bit)
        bit *= 2
        kept_rows = width + LEVEL_ROWS if bit < n_seq else width
        mixed = combine(flip, mixed, other, kept_rows, after)
    far_mixed = swap(mixed, "tp", 2)
    near_mixed = swap(mixed, "tp", 1)

    core = tp_index & 1
    side = tp_index >> 1
    vocab = pltpu.with_memory_space_constraint(w_vocab.T, pltpu.HBM)
    limit = vocab.shape[0]
    vocab_rows = pl.cdiv(limit, 4 * 32) * 64
    away = (vocab_rows * (1 - core)).reshape(1)
    far_gain, own_weight = pinned([last_gain, w_split])
    held, field = begin_rows(
        away, vocab, own_weight, all_tokens[-1], mixed, near_mixed, w_parts[1]
    )
    relayed, far_mixed = call(
        twice_body, [struct(far_mixed.shape, BF16)] * 2, [], [far_mixed], (field,)
    )
    last_mixed = swap(relayed, "tp", 1)
    squares, scaled, again = call(
        rows_body,
        [struct((1, requests), F32)] + [struct(own_tokens.shape, BF16)] * 2,
        [],
        [field, far_mixed, last_mixed, *w_parts[2:]],
        scratch=[pltpu.VMEM((columns, 1), F32), pltpu.SemaphoreType.DMA((1,))],
        far=[far_gain],
    )
    (sent,) = call(
        partial(held_body, limit),
        [struct((vocab_rows, requests), BF16)],
        [away],
        [held, scaled],
    )
    kept = half_logits((2 * core).reshape(1), vocab, again, (sent,))
    quarter = kept.shape[0] // 2
    sent, kept = call(
        fold_body,
        [struct((quarter, requests), BF16), struct((quarter, requests), F32)],
        [side.reshape(1)],
        [kept, swap(sent, "tp", 1)],
    )
    state = ()
    while sources:
        last = len(sources) <= 4
        state = attend(
            sources[:4], last, seq_index.reshape(1), low, query, blocks[:4], state, 30
        )
        sources, blocks = sources[4:], blocks[4:]
    (best,) = call(
        top_body, [struct((1, requests), F32)], [], [kept, swap(sent, "tp", 2)], state[:1]
    )
    bit = 1
    while bit < n_seq:
        best = jnp.maximum(best, swap(best, "seq", bit))
        bit *= 2
    attended = spread(state[0])
    (pair,) = call(
        pair_body, [struct((2, requests), F32)], [], [best, squares], attended[2:3]
    )
    other = swap(pair, "tp", 2)
    pair = jnp.stack([jnp.maximum(pair[0], other[0]), pair[1] + other[1]])
    summed = sum(
        mm_last(part, w).astype(BF16).astype(F32) for part, w in zip(attended, w_parts)
    )
    hidden = (tokens.astype(F32) + summed).astype(BF16)
    (pair,) = call(
        join_body, [struct((2, requests), F32)], [], [pair, swap(pair, "tp", 1)], (hidden,)
    )
    hidden_norm = jnp.sqrt(pair[1] / D + EPS)
    top_logit = pair[0] / hidden_norm * (1.0 / SHRINK)
    return (kv_cache, hidden, hidden_norm, top_logit)


def solution(mesh):
    return jax.shard_map(
        shards,
        mesh=mesh,
        in_specs=(
            P("seq", "tp"),
            P(),
            P(None, "tp"),
            P(None, "tp"),
            P(None, "tp"),
            P("tp", None),
            P("tp"),
            P("tp", "seq"),
            P("seq"),
            P(),
            P(),
        ),
        out_specs=(P("tp", "seq", None), P("seq", "tp"), P(), P()),
        check_vma=False,
    )
```
